512 devices in a mesh: col: 16 (over x, y), row: 32 (over z, core).
Axes of the slice: x: 4, y: 4, z: 16, core: 2. Of those that a mesh axis runs over, the one named last changes fastest.
Arguments:
- features: bfloat16 [65536, 256], P(('col', 'row')), may hold values from -6 to 6
- weight: bfloat16 [256, 256], replicated, may hold values from -0.375 to 0.375
- grad_out: bfloat16 [65536, 256], P(('col', 'row')), may hold values from -6 to 6
- tile_values: bfloat16 [16, 32, 96, 128, 128], P('col', 'row'), may hold values from -0.078125 to 0.078125
- tile_coords: int32 [16, 32, 2, 96], P('col', 'row'), may hold values from 0 to 31, as said below
- tile_count: int32 [16, 32], P('col', 'row'), may hold values from 1 to 96, as said below
Outputs:
- feature_grad: bfloat16 [65536, 256], P(('col', 'row'))
- weight_grad: float32 [256, 256], replicated
The draws below stay inside these ranges and needn't reach their ends.
Inputs may be any that keep to these rules, and one draw needn't show every extreme that they name: tile_coords[c, r, 0, k] is below 16 and tile_coords[c, r, 1, k] below 32; the 96 pairs of one block are all different. `tile_count`: at least one block has exactly 96 live slots.
All inputs are finite; a program needn't handle non-finite values.
Results may differ from the reference program's by a relative error of at most 0.03.
Values may be sent and summed in bfloat16 or wider, within the bound.
A program may use at most 64 MiB of HBM per device.

```python
import math
import jax
import jax.numpy as jnp
from jax import lax

F = 256
TILE = 128
NODE_DEV = 128
NODES = 65536
ROW_TILES = 16
COL_TILES = 32
TGRID = 512
SLOTS = 96
N_COL = 16
N_ROW = 32


def draw_tile_coords(key, part):
    key = jax.random.fold_in(key, 11)
    block_keys = jax.random.split(key, N_COL * N_ROW)

    def one_block(block_key):
        chosen = jax.random.permutation(block_key, TGRID)[:SLOTS].astype(jnp.int32)
        return jnp.stack([chosen // COL_TILES, chosen % COL_TILES])
    pairs = jax.vmap(one_block)(block_keys)
    return pairs.reshape(N_COL, N_ROW, 2, SLOTS).astype(jnp.int32)


def draw_tile_count(key, part):
    key = jax.random.fold_in(key, 12)
    first_key, second_key, third_key = jax.random.split(key, 3)
    lowest = max(1, SLOTS // 8)
    first_draw = jax.random.randint(first_key, (N_COL * N_ROW,), lowest, SLOTS + 1)
    second_draw = jax.random.randint(second_key, (N_COL * N_ROW,), lowest, SLOTS + 1)
    counts = jnp.minimum(first_draw, second_draw)
    fullest = jax.random.randint(third_key, (), 0, N_COL * N_ROW)
    counts = counts.at[fullest].set(SLOTS)
    return counts.reshape(N_COL, N_ROW).astype(jnp.int32)


def levels(own_key, extent, cuts, least, largest):
    factor_of = 1.0
    for axis_at, parts in cuts:
        steps = jax.random.uniform(jax.random.fold_in(jax.random.fold_in(own_key, 6), axis_at), (parts,), jnp.float32, least / len(cuts), largest / len(cuts))
        factor_of = factor_of * jnp.repeat(jnp.exp(steps), extent[axis_at] // parts).reshape((-1,) + (1,) * (len(extent) - 1 - axis_at))
    return factor_of


def gaussian(own_key, dims, spread, bound, shards=(), held_as=jnp.bfloat16):
    factor_of = levels(own_key, dims, shards, -0.22, 0.18) if shards else 1.0
    drawn = jax.random.normal(own_key, dims, jnp.float32) * spread * factor_of
    return jnp.minimum(jnp.maximum(drawn, -bound), bound).astype(held_as)


def setup_inputs(seed: int = 0) -> dict:
    key_list = jax.random.split(jax.random.key(seed), 7)
    return {
        "features": gaussian(key_list[0], (NODES, F), 1.0, 6.0, ((0, 512),)),
        "weight": gaussian(key_list[1], (F, F), F ** -0.5, 0.375),
        "grad_out": gaussian(key_list[2], (NODES, F), 1.0, 6.0, ((0, 512),)),
        "tile_values": gaussian(key_list[3], (N_COL, N_ROW, SLOTS, TILE, TILE), (SLOTS * TILE * TILE // (2 * NODE_DEV)) ** -0.5, 0.078125, ((0, 16), (1, 32))),
        "tile_coords": draw_tile_coords(jax.random.fold_in(key_list[6], 71), 0),
        "tile_count": draw_tile_count(jax.random.fold_in(key_list[6], 71), 0),
    }


def forward_block(tile_block, tile_pairs, live_count, column_rows):
    slot_count = tile_block.shape[0]
    live_slots = (jnp.arange(slot_count) < live_count).astype(jnp.bfloat16)
    masked = (tile_block * live_slots[:, None, None]).astype(jnp.float32)
    picked = column_rows.reshape(COL_TILES, TILE, F)[tile_pairs[1]].astype(jnp.float32)
    product = jnp.einsum('sab,sbf->saf', masked, picked, precision=lax.Precision.HIGHEST)
    onehot = (tile_pairs[0][None, :] == jnp.arange(ROW_TILES)[:, None]).astype(jnp.float32)
    summed = jnp.einsum('ts,saf->taf', onehot, product, precision=lax.Precision.HIGHEST)
    return summed.reshape(ROW_TILES * TILE, F).astype(jnp.bfloat16)

def backward_block(tile_block, tile_pairs, live_count, block_rows):
    slot_count = tile_block.shape[0]
    live_slots = (jnp.arange(slot_count) < live_count).astype(jnp.bfloat16)
    masked = (tile_block * live_slots[:, None, None]).astype(jnp.float32)
    picked = block_rows.reshape(ROW_TILES, TILE, F)[tile_pairs[0]].astype(jnp.float32)
    product = jnp.einsum('sab,saf->sbf', masked, picked, precision=lax.Precision.HIGHEST)
    onehot = (tile_pairs[1][None, :] == jnp.arange(COL_TILES)[:, None]).astype(jnp.float32)
    summed = jnp.einsum('ts,sbf->tbf', onehot, product, precision=lax.Precision.HIGHEST)
    return summed.reshape(COL_TILES * TILE, F).astype(jnp.bfloat16)

def reference(features, weight, grad_out, tile_values, tile_coords, tile_count):
    column_groups = features.reshape(N_COL, N_ROW * NODE_DEV, F)

    def forward_col(running, col_index):

        def device_part(row_index):
            return forward_block(tile_values[col_index, row_index], tile_coords[col_index, row_index], tile_count[col_index, row_index], column_groups[col_index])
        partials = lax.map(device_part, jnp.arange(N_ROW))
        return (running + partials.astype(jnp.float32), None)
    start_rows = jnp.zeros((N_ROW, ROW_TILES * TILE, F), jnp.float32)
    row_sums, _ = lax.scan(forward_col, start_rows, jnp.arange(N_COL))
    agg = row_sums.astype(jnp.bfloat16).reshape(N_ROW, N_COL, NODE_DEV, F)
    agg = jnp.transpose(agg, (1, 0, 2, 3)).reshape(NODES, F)
    pre_act = jnp.dot(agg, weight, preferred_element_type=jnp.float32)
    sigmoid_z = jax.nn.sigmoid(pre_act)
    dz = (grad_out.astype(jnp.float32) * (sigmoid_z * (1.0 + pre_act * (1.0 - sigmoid_z)))).astype(jnp.bfloat16)
    back = jnp.dot(dz, weight.T, preferred_element_type=jnp.float32).astype(jnp.bfloat16)
    weight_grad = jnp.dot(agg.T, dz, preferred_element_type=jnp.float32) * (1.0 / math.sqrt(NODES))
    row_groups = jnp.transpose(back.reshape(N_COL, N_ROW, NODE_DEV, F), (1, 0, 2, 3))
    row_groups = row_groups.reshape(N_ROW, N_COL * NODE_DEV, F)

    def backward_row(running, row_index):

        def device_part(col_index):
            return backward_block(tile_values[col_index, row_index], tile_coords[col_index, row_index], tile_count[col_index, row_index], row_groups[row_index])
        partials = lax.map(device_part, jnp.arange(N_COL))
        return (running + partials.astype(jnp.float32), None)
    start_cols = jnp.zeros((N_COL, COL_TILES * TILE, F), jnp.float32)
    col_sums, _ = lax.scan(backward_row, start_cols, jnp.arange(N_ROW))
    feature_grad = col_sums.reshape(NODES, F).astype(jnp.bfloat16)
    return (feature_grad, weight_grad)
```

```python
import functools
import math

import jax
import jax.numpy as jnp
from jax import lax
from jax.experimental import pallas as pl
from jax.experimental.pallas import tpu as pltpu
from jax.sharding import PartitionSpec as P

MESH = pl.DeviceIdType.MESH
DMA = pltpu.SemaphoreType.DMA
BF = jnp.bfloat16
F32 = jnp.float32

SX, SY, SZ = 4, 4, 16
OFFS = (0, 1, -1, 2, -2, 3, -3, 4, -4, 5, -5, 6, -6, 7, -7, 8)
GROUPS = ((0, 1), (1, 5), (5, 9), (9, 13), (13, 16))
SLOT = {o: t for t, o in enumerate(OFFS)}
SLOT[-8] = SLOT[8]
NCOL = SX * SY


class Links:
    def __init__(self, send_sems, recv_sems):
        self.send_sems, self.recv_sems = send_sems, recv_sems
        self.used = 0
        self.sent = []

    def copy(self, src, dst, device):
        at = self.used
        self.used += 1
        return pltpu.make_async_remote_copy(
            src_ref=src,
            dst_ref=dst,
            send_sem=self.send_sems.at[at],
            recv_sem=self.recv_sems.at[at],
            device_id=device,
            device_id_type=MESH,
        )

    def start(self, src, dst, device):
        copy = self.copy(src, dst, device)
        copy.start()
        self.sent.append(copy)
        return copy

    def drain(self):
        for copy in self.sent:
            copy.wait_send()


def kernel(
    pieces,
    scaling,
    coords_ref,
    count_ref,
    feat_ref,
    weight_ref,
    grad_ref,
    tiles_ref,
    out_ref,
    wout_ref,
    inv_v,
    inv_s,
    tiles,
    tiles_t,
    feats,
    acc,
    part,
    part_rx,
    backs,
    own_t,
    pair_tx,
    pair_rx,
    leaf_tx,
    leaf_rx,
    chain_tx,
    chain_rx,
    w_loc,
    w_pair,
    w_sum,
    w_rx,
    w_z,
    w_piece,
    w_fin,
    local_sems,
    send_sems,
    recv_sems,
):
    col, row = lax.axis_index("col"), lax.axis_index("row")
    x, y = col // SY, col % SY
    z, core = row // 2, row % 2
    links = Links(send_sems, recv_sems)
    slots = tiles_ref.shape[0]
    tile = tiles_ref.shape[1]
    half = tile // 2

    def at_z(offset):
        return (col, lax.rem(z + offset + SZ, SZ) * 2 + core)

    def col_at(dx, dy):
        return lax.rem(x + dx + SX, SX) * SY + lax.rem(y + dy + SY, SY)

    partner = (col, z * 2 + 1 - core)
    shifts = [(d // SY, d % SY) for d in range(1, NCOL)]

    barrier = pltpu.get_barrier_semaphore()
    greeted = [at_z(o) for o in (1, -1, 2, -2)] + [partner]
    greeted += [(col_at(dx, dy), row) for dx, dy in shifts]
    for device in greeted:
        pl.semaphore_signal(barrier, inc=1, device_id=device, device_id_type=MESH)

    load_tiles = pltpu.make_async_copy(
        tiles_ref, tiles.at[pl.ds(1, slots)], local_sems.at[0]
    )
    load_tiles.start()
    feats[0, 0] = feat_ref[...]
    pl.semaphore_wait(barrier, len(greeted))

    ahead = {}
    rows_of = tile // pieces

    def rows(p):
        return pl.ds(p * rows_of, rows_of)

    def forward(buf, key, dist, side, p, whole):
        src = SLOT[side * dist]
        for hop in (2, 1):
            far = dist + hop
            if far > 8:
                continue
            if far == 8 and (p < whole // 2) != (side == 1):
                continue
            dst = SLOT[side * far]
            ahead[key, side * far, p] = links.start(
                buf(src, p), buf(dst, p), at_z(side * hop)
            )

    def feat_at(t, p):
        return feats.at[t, 0, rows(p)]

    crossed = {}

    def cross(t, p):
        crossed[t, p] = links.start(
            feats.at[t, 0, rows(p)], feats.at[t, 1, rows(p)], partner
        )

    for p in range(pieces):
        for side in (1, -1):
            forward(feat_at, "f", 0, side, p, pieces)
    for p in range(pieces):
        cross(0, p)

    tile_row = lax.broadcasted_iota(jnp.int32, inv_v.shape, 0)
    tile_col = lax.broadcasted_iota(jnp.int32, inv_v.shape, 1)
    live = count_ref[0, 0]

    def enter(k, table):
        hit = (tile_row == coords_ref[0, k]) & (tile_col == coords_ref[1, k])
        hit = hit & (jnp.full(inv_v.shape, k, jnp.int32) < live)
        return jnp.where(hit, k + 1, table)

    inv_v[...] = lax.fori_loop(
        0, slots, enter, jnp.zeros(inv_v.shape, jnp.int32), unroll=8
    )
    table_copy = pltpu.make_async_copy(inv_v, inv_s, local_sems.at[1])
    table_copy.start()
    tiles[0] = jnp.zeros(tiles.shape[1:], BF)
    tiles_t[0] = jnp.zeros(tiles.shape[1:], BF)
    table_copy.wait()
    load_tiles.wait()

    def column_tile(t, other):
        source = lax.rem(z - OFFS[t] + SZ, SZ)
        return source * 2 + (1 - core if other else core)

    block = 4

    def row_tile_of(q):
        d = NCOL - 1 - q
        return lax.rem(x + d // SY, SX) * SY + lax.rem(y + d % SY, SY)

    def product(lo, hi, q0):
        columns = [column_tile(t, o) for t in range(lo, hi) for o in (0, 1)]
        lhs = []
        for a in range(block):
            i = row_tile_of(q0 + a)
            lhs.append(jnp.concatenate([tiles[inv_s[i, j]] for j in columns], axis=1))
        rhs = feats[lo:hi].reshape((hi - lo) * 2 * tile, -1)
        return jnp.dot(
            jnp.concatenate(lhs, axis=0), rhs, preferred_element_type=F32
        )

    def accumulate(lo, hi):
        def one(b, carry):
            at = pl.ds(pl.multiple_of(b * block * tile, block * tile), block * tile)
            if lo == 0:
                acc[at] = product(lo, hi, b * block)
            else:
                acc[at] += product(lo, hi, b * block)
            return carry

        lax.fori_loop(0, NCOL // block, one, 0)

    def flip(k, carry):
        tiles_t[k + 1] = tiles[k + 1].T
        return carry

    for s, (lo, hi) in enumerate(GROUPS):
        if s:
            for p in range(pieces):
                for side in (1, -1):
                    key = ("f", side * 2 * s, p)
                    if key in ahead:
                        ahead[key].wait_recv()
                        if s < 4:
                            forward(feat_at, "f", 2 * s, side, p, pieces)
                        cross(SLOT[side * 2 * s], p)
                for side in (1, -1):
                    ahead["f", side * (2 * s - 1), p].wait_recv()
                    cross(SLOT[side * (2 * s - 1)], p)
            before_lo, before_hi = GROUPS[s - 1]
        else:
            lax.fori_loop(0, slots, flip, 0, unroll=4)
            continue
        for t in range(before_lo, before_hi):
            for p in range(pieces):
                crossed[t, p].wait_recv()
        accumulate(before_lo, before_hi)

    lo, hi = GROUPS[-1]
    for t in range(lo, hi):
        for p in range(pieces):
            crossed[t, p].wait_recv()

    arrivals = {}
    for b in range(NCOL // block):
        at = pl.ds(b * block * tile, block * tile)
        total = acc[at] + product(lo, hi, b * block)
        acc[at] = total
        for a in range(block):
            q = b * block + a
            d = NCOL - 1 - q
            if d:
                part[d - 1] = total[a * tile : (a + 1) * tile].astype(BF)
                arrivals[d] = links.start(
                    part.at[d - 1],
                    part_rx.at[d - 1],
                    (col_at(d // SY, d % SY), row),
                )
    agg = acc[pl.ds((NCOL - 1) * tile, tile)]
    for d in range(NCOL - 1, 0, -1):
        arrivals[d].wait_recv()
        agg = agg + part_rx[d - 1].astype(F32)
    agg = agg.astype(BF)

    weight = weight_ref[...]
    pre_act = jnp.dot(agg, weight, preferred_element_type=F32)
    sigmoid_z = jax.nn.sigmoid(pre_act)
    factor = sigmoid_z * (1.0 + pre_act * (1.0 - sigmoid_z))
    dz = (grad_ref[...].astype(F32) * factor).astype(BF)
    backs[0] = lax.dot_general(
        dz, weight, (((1,), (1,)), ((), ())), preferred_element_type=F32
    ).astype(BF)
    for d in range(NCOL - 1, 0, -1):
        arrivals[d] = links.start(
            backs.at[0], backs.at[d], (col_at(d // SY, d % SY), row)
        )
    local_weight = lax.dot_general(
        agg, dz, (((0,), (0,)), ((), ())), preferred_element_type=F32
    )
    for h in range(2):
        w_loc[h] = local_weight[:, h * 128 : (h + 1) * 128].reshape(NCOL, -1, 128)

    w_cross = links.start(w_loc.at[1 - core], w_pair, partner)
    w_cross.wait_recv()
    w_sum[...] = w_loc[core] + w_pair[...]
    w_arrivals = {}
    for d in range(NCOL - 1, 0, -1):
        to = col_at(d // SY, d % SY)
        w_arrivals[d] = links.start(w_sum.at[to], w_rx.at[d - 1], (to, row))

    for d in range(NCOL - 1, 0, -1):
        arrivals[d].wait_recv()

    def back_tile_of(d):
        return lax.rem(x - d // SY + SX, SX) * SY + lax.rem(y - d % SY + SY, SY)

    def transposed(columns):
        lhs = []
        for j in columns:
            lhs.append(
                jnp.concatenate(
                    [tiles_t[inv_s[back_tile_of(d), j]] for d in range(NCOL)], axis=1
                )
            )
        return jnp.dot(
            jnp.concatenate(lhs, axis=0),
            backs[...].reshape(NCOL * tile, -1),
            preferred_element_type=F32,
        )

    pair = {}

    def compute(offsets):
        for t0 in range(0, len(offsets), 2):
            some = offsets[t0 : t0 + 2]
            targets = [lax.rem(z + o + SZ, SZ) * 2 for o in some]
            terms = transposed(
                [t + 1 - core for t in targets] + [t + core for t in targets]
            )
            for n, o in enumerate(some):
                t = SLOT[o]
                pair_tx[t] = terms[n * tile : (n + 1) * tile].astype(BF)
                pair[t] = links.start(pair_tx.at[t], pair_rx.at[t], partner)
                m = n + len(some)
                own_t[t] = terms[m * tile : (m + 1) * tile]

    def pair_sum(o):
        t = SLOT[o]
        pair[t].wait_recv()
        return own_t[t] + pair_rx[t].astype(F32)

    leaf, chain = {}, {}

    def send_leaves(dist):
        for n, side in enumerate((1, -1)):
            m = dist // 2
            leaf_tx[n, m] = pair_sum(side * dist).astype(BF)
            leaf[side, dist] = links.start(
                leaf_tx.at[n, m], leaf_rx.at[n, m], at_z(side)
            )

    def send_chain(dist):
        m = dist // 2 - 1
        if dist == 8:
            total = pair_sum(8).astype(BF)
            for n, side in enumerate((1, -1)):
                chain_tx[n, m, n * half : (n + 1) * half] = total[
                    n * half : (n + 1) * half
                ]
                chain[side, dist] = links.start(
                    chain_tx.at[n, m, pl.ds(n * half, half)],
                    chain_rx.at[n, m, pl.ds(n * half, half)],
                    at_z(2 * side),
                )
            return
        for n, side in enumerate((1, -1)):
            total = pair_sum(side * dist)
            leaf[side, dist + 1].wait_recv()
            total = total + leaf_rx[n, m + 1].astype(F32)
            chain[side, dist + 2].wait_recv()
            if dist == 6:
                mine = total[n * half : (n + 1) * half]
                mine = mine + chain_rx[n, m + 1, n * half : (n + 1) * half].astype(F32)
                rest = total[(1 - n) * half : (2 - n) * half]
                chain_tx[n, m, n * half : (n + 1) * half] = mine.astype(BF)
                chain_tx[n, m, (1 - n) * half : (2 - n) * half] = rest.astype(BF)
            else:
                total = total + chain_rx[n, m + 1].astype(F32)
                chain_tx[n, m] = total.astype(BF)
            chain[side, dist] = links.start(
                chain_tx.at[n, m], chain_rx.at[n, m], at_z(2 * side)
            )

    def w_at(t, p):
        return w_z.at[t]

    def w_round(s):
        for side in (1, -1):
            key = ("w", side * 2 * s, 0)
            if key in ahead:
                ahead[key].wait_recv()
                if s < 4:
                    forward(w_at, "w", 2 * s, side, 0, 1)
            ahead["w", side * (2 * s - 1), 0].wait_recv()

    compute([8, 7, -7])
    compute([6, -6, 5, -5])
    send_leaves(7)
    send_chain(8)
    w_total = w_sum[col]
    for d in range(NCOL - 1, 0, -1):
        w_arrivals[d].wait_recv()
        w_total = w_total + w_rx[d - 1]
    w_z[0] = w_total.astype(BF)
    for side in (1, -1):
        forward(w_at, "w", 0, side, 0, 1)
    send_leaves(5)
    compute([4, -4, 3, -3])
    compute([2, -2, 1, -1])
    send_leaves(3)
    send_chain(6)
    w_round(1)
    compute([0])
    send_leaves(1)
    w_round(2)
    send_chain(4)
    w_round(3)
    send_chain(2)
    w_round(4)
    w_total = w_z[0].astype(F32)
    for t in range(1, len(OFFS)):
        w_total = w_total + w_z[t].astype(F32)
    w_fin[core, col] = w_total * scaling
    for d in range(NCOL - 1, 0, -1):
        to = col_at(d // SY, d % SY)
        w_arrivals[d] = links.start(w_fin.at[core, col], w_fin.at[core, col], (to, row))
    total = pair_sum(0)
    for n, side in enumerate((1, -1)):
        leaf[side, 1].wait_recv()
        total = total + leaf_rx[n, 0].astype(F32)
    for n, side in enumerate((1, -1)):
        chain[side, 2].wait_recv()
        total = total + chain_rx[n, 0].astype(F32)
    out_ref[...] = total.astype(BF)
    for d in range(NCOL - 1, 0, -1):
        w_arrivals[d].wait_recv()
    w_cross = links.start(w_fin.at[core], w_fin.at[core], partner)
    w_cross.wait_recv()
    for h in range(2):
        wout_ref[:, h * 128 : (h + 1) * 128] = w_fin[h].reshape(-1, 128)
    links.drain()


PIECES = 2
COPIES = 256


def body(features, weight, grad_out, tile_values, tile_coords, tile_count):
    tile, width = features.shape
    slots = tile_values.shape[2]
    nodes = tile * lax.axis_size("col") * lax.axis_size("row")
    vmem = pl.BlockSpec(memory_space=pltpu.VMEM)
    smem = pl.BlockSpec(memory_space=pltpu.SMEM)
    square = (tile, tile)
    slab = (tile, width)
    w_rows = width // NCOL
    return pl.pallas_call(
        functools.partial(kernel, PIECES, 1.0 / math.sqrt(nodes)),
        out_shape=(
            jax.ShapeDtypeStruct(slab, BF),
            jax.ShapeDtypeStruct((width, width), F32),
        ),
        in_specs=[smem, smem, vmem, vmem, vmem, pl.BlockSpec(memory_space=pl.ANY)],
        out_specs=(vmem, vmem),
        scratch_shapes=[
            pltpu.VMEM((16, 128), jnp.int32),
            pltpu.SMEM((16, 128), jnp.int32),
            pltpu.VMEM((slots + 1,) + square, BF),
            pltpu.VMEM((slots + 1,) + square, BF),
            pltpu.VMEM((16, 2) + slab, BF),
            pltpu.VMEM((NCOL * tile, width), F32),
            pltpu.VMEM((NCOL - 1,) + slab, BF),
            pltpu.VMEM((NCOL - 1,) + slab, BF),
            pltpu.VMEM((NCOL,) + slab, BF),
            pltpu.VMEM((16,) + slab, F32),
            pltpu.VMEM((16,) + slab, BF),
            pltpu.VMEM((16,) + slab, BF),
            pltpu.VMEM((2, 4) + slab, BF),
            pltpu.VMEM((2, 4) + slab, BF),
            pltpu.VMEM((2, 4) + slab, BF),
            pltpu.VMEM((2, 4) + slab, BF),
            pltpu.VMEM((2, NCOL, w_rows, 128), F32),
            pltpu.VMEM((NCOL, w_rows, 128), F32),
            pltpu.VMEM((NCOL, w_rows, 128), F32),
            pltpu.VMEM((NCOL - 1, w_rows, 128), F32),
            pltpu.VMEM((16, w_rows, 128), BF),
            pltpu.VMEM((w_rows, 128), F32),
            pltpu.VMEM((2, NCOL, w_rows, 128), F32),
            DMA((2,)),
            DMA((COPIES,)),
            DMA((COPIES,)),
        ],
        compiler_params=pltpu.CompilerParams(
            collective_id=0, has_side_effects=True, vmem_limit_bytes=56 << 20
        ),
        name="layer_backward",
    )(
        tile_coords[0, 0],
        tile_count,
        features,
        weight,
        grad_out,
        tile_values[0, 0],
    )


def solution(mesh):
    return jax.shard_map(
        body,
        mesh=mesh,
        in_specs=(
            P(("col", "row"), None),
            P(),
            P(("col", "row"), None),
            P("col", "row", None, None, None),
            P("col", "row", None, None),
            P("col", "row"),
        ),
        out_specs=(P(("col", "row"), None), P()),
        check_vma=False,
    )
```

```python
import functools
import math

import jax
import jax.numpy as jnp
from jax import lax
from jax.experimental import pallas as pl
from jax.experimental.pallas import tpu as pltpu
from jax.sharding import PartitionSpec as P

MESH = pl.DeviceIdType.MESH
DMA = pltpu.SemaphoreType.DMA
BF = jnp.bfloat16
F32 = jnp.float32

SX, SY, SZ = 4, 4, 16
OFFS = (0, 1, -1, 2, -2, 3, -3, 4, -4, 5, -5, 6, -6, 7, -7, 8)
GROUPS = ((0, 1), (1, 5), (5, 9), (9, 13), (13, 16))
SLOT = {o: t for t, o in enumerate(OFFS)}
SLOT[-8] = SLOT[8]
NCOL = SX * SY


class Links:
    def __init__(self, send_sems, recv_sems):
        self.send_sems, self.recv_sems = send_sems, recv_sems
        self.used = 0
        self.sent = []

    def copy(self, src, dst, device):
        at = self.used
        self.used += 1
        return pltpu.make_async_remote_copy(
            src_ref=src,
            dst_ref=dst,
            send_sem=self.send_sems.at[at],
            recv_sem=self.recv_sems.at[at],
            device_id=device,
            device_id_type=MESH,
        )

    def start(self, src, dst, device):
        copy = self.copy(src, dst, device)
        copy.start()
        self.sent.append(copy)
        return copy

    def drain(self):
        for copy in self.sent:
            copy.wait_send()


def kernel(
    pieces,
    scaling,
    coords_ref,
    count_ref,
    feat_ref,
    weight_ref,
    grad_ref,
    tiles_ref,
    out_ref,
    wout_ref,
    inv_v,
    inv_s,
    tiles,
    tiles_t,
    feats,
    acc,
    part,
    part_rx,
    sums,
    sums_rx,
    backs,
    own_t,
    pair_tx,
    pair_rx,
    leaf_tx,
    leaf_rx,
    chain_tx,
    chain_rx,
    w_loc,
    w_rx,
    w_sum,
    w_rx2,
    w_far,
    w_near,
    w_pair,
    w_fin,
    local_sems,
    send_sems,
    recv_sems,
):
    col, row = lax.axis_index("col"), lax.axis_index("row")
    x, y = col // SY, col % SY
    z, core = row // 2, row % 2
    links = Links(send_sems, recv_sems)
    slots = tiles_ref.shape[0]
    tile = tiles_ref.shape[1]
    half = tile // 2

    def at_z(offset):
        return (col, lax.rem(z + offset + SZ, SZ) * 2 + core)

    def col_at(dx, dy):
        return lax.rem(x + dx + SX, SX) * SY + lax.rem(y + dy + SY, SY)

    partner = (col, z * 2 + 1 - core)

    def beside(axis, offset):
        return (col_at(offset, 0) if axis == 0 else col_at(0, offset), row)

    barrier = pltpu.get_barrier_semaphore()
    greeted = [at_z(o) for o in (1, -1, 2, -2, 4, -4, 8)] + [partner]
    greeted += [beside(axis, o) for axis in (0, 1) for o in (1, 2, 3)]
    for device in greeted:
        pl.semaphore_signal(barrier, inc=1, device_id=device, device_id_type=MESH)

    load_tiles = pltpu.make_async_copy(
        tiles_ref, tiles.at[pl.ds(1, slots)], local_sems.at[0]
    )
    load_tiles.start()
    feats[0, 0] = feat_ref[...]
    pl.semaphore_wait(barrier, len(greeted))

    ahead = {}
    rows_of = tile // pieces

    def rows(p):
        return pl.ds(p * rows_of, rows_of)

    def feat_at(t, p):
        return feats.at[t, 0, rows(p)]

    def stride(dist):
        for p in range(pieces):
            for side in (1, -1):
                far = dist + 2
                if dist:
                    ahead[side * dist, p].wait_recv()
                if far == 8 and (p < pieces // 2) != (side == 1):
                    continue
                ahead[side * far, p] = links.start(
                    feat_at(SLOT[side * dist], p),
                    feat_at(SLOT[side * far], p),
                    at_z(side * 2),
                )

    def hand_over(dist):
        for side in (1, -1):
            ahead[side * (dist + 1)] = links.start(
                feats.at[SLOT[side * dist], 0],
                feats.at[SLOT[side * (dist + 1)], 0],
                at_z(side),
            )

    crossed = {}

    def cross(t):
        crossed[t] = links.start(feats.at[t, 0], feats.at[t, 1], partner)

    stride(0)
    hand_over(0)
    cross(0)

    tile_row = lax.broadcasted_iota(jnp.int32, inv_v.shape, 0)
    tile_col = lax.broadcasted_iota(jnp.int32, inv_v.shape, 1)
    live = jnp.broadcast_to(count_ref[...], inv_v.shape)

    def enter(k, table):
        hit = (tile_row == coords_ref[0, k]) & (tile_col == coords_ref[1, k])
        hit = hit & (jnp.full(inv_v.shape, k, jnp.int32) < live)
        return jnp.where(hit, k + 1, table)

    inv_v[...] = lax.fori_loop(
        0, slots, enter, jnp.zeros(inv_v.shape, jnp.int32), unroll=8
    )
    table_copy = pltpu.make_async_copy(inv_v, inv_s, local_sems.at[1])
    table_copy.start()
    tiles[0] = jnp.zeros(tiles.shape[1:], BF)
    tiles_t[0] = jnp.zeros(tiles.shape[1:], BF)
    table_copy.wait()
    load_tiles.wait()

    def column_tile(t, other):
        source = lax.rem(z - OFFS[t] + SZ, SZ)
        return source * 2 + (1 - core if other else core)

    block = 4

    order = [
        (a + i, b + j) for a, b in ((2, 2), (2, 0), (0, 2), (0, 0)) for i in (0, 1) for j in (0, 1)
    ]

    def row_tile_of(q):
        a = 2 - 2 * (q // 8) + q % 4 // 2
        b = 2 - 2 * (q // 4 % 2) + q % 2
        return lax.rem(x + a, SX) * SY + lax.rem(y + b, SY)

    def product(lo, hi, q0):
        columns = [column_tile(t, o) for t in range(lo, hi) for o in (0, 1)]
        lhs = []
        for a in range(block):
            i = row_tile_of(q0 + a)
            lhs.append(jnp.concatenate([tiles[inv_s[i, j]] for j in columns], axis=1))
        rhs = feats[lo:hi].reshape((hi - lo) * 2 * tile, -1)
        return jnp.dot(
            jnp.concatenate(lhs, axis=0), rhs, preferred_element_type=F32
        )

    def accumulate(lo, hi):
        def one(b, carry):
            at = pl.ds(pl.multiple_of(b * block * tile, block * tile), block * tile)
            if lo == 0:
                acc[at] = product(lo, hi, b * block)
            else:
                acc[at] += product(lo, hi, b * block)
            return carry

        lax.fori_loop(0, NCOL // block, one, 0)

    def flip(k, carry):
        tiles_t[k + 1] = tiles[k + 1].T
        return carry

    lax.fori_loop(0, slots, flip, 0, unroll=4)
    for s in range(1, 5):
        if s < 4:
            stride(2 * s)
            hand_over(2 * s)
        else:
            for p in range(pieces):
                ahead[8 if p < pieces // 2 else -8, p].wait_recv()
        for side in (1, -1):
            if s < 4:
                cross(SLOT[side * 2 * s])
            ahead[side * (2 * s - 1)].wait_recv()
            cross(SLOT[side * (2 * s - 1)])
        if s == 4:
            cross(SLOT[8])
        lo, hi = GROUPS[s - 1]
        for t in range(lo, hi):
            crossed[t].wait_recv()
        accumulate(lo, hi)

    lo, hi = GROUPS[-1]
    for t in range(lo, hi):
        crossed[t].wait_recv()

    lanes = [slice(0, 128), slice(128, 256)]
    first = {}
    for b in range(NCOL // block):
        at = pl.ds(b * block * tile, block * tile)
        total = (acc[at] + product(lo, hi, b * block)).astype(BF)
        some = order[b * block : (b + 1) * block]
        for n, (dx, dy) in enumerate(some):
            for axis, (i, w) in enumerate(((dx, dy), (dy, dx))):
                part[axis, i, w] = total[n * tile : (n + 1) * tile, lanes[axis]]
        for axis in (0, 1):
            for i in sorted({d[axis] for d in some}):
                w = min(d[1 - axis] for d in some)
                if i:
                    first[axis, i, w] = links.start(
                        part.at[axis, i, pl.ds(w, 2)],
                        part_rx.at[axis, i, pl.ds(w, 2)],
                        beside(axis, i),
                    )
    second = {}
    own_sum = {}
    for w0 in (2, 0):
        for axis in (0, 1):
            for i in (1, 2, 3):
                first[axis, i, w0].wait_recv()
            for w in (w0 + 1, w0) if w0 == 0 else (w0, w0 + 1):
                mine = part[axis, 0, w].astype(F32)
                for i in (1, 2, 3):
                    mine = mine + part_rx[axis, i, w].astype(F32)
                if w:
                    sums[axis, w] = mine.astype(BF)
                    second[axis, w] = links.start(
                        sums.at[axis, w], sums_rx.at[axis, w], beside(1 - axis, w)
                    )
                else:
                    own_sum[axis] = mine
    halves = []
    for axis in (0, 1):
        mine = own_sum[axis]
        for w in (2, 3, 1):
            second[axis, w].wait_recv()
            mine = mine + sums_rx[axis, w].astype(F32)
        halves.append(mine)
    agg = jnp.concatenate(halves, axis=1)
    agg = agg.astype(BF)

    weight = weight_ref[...]
    pre_act = jnp.dot(agg, weight, preferred_element_type=F32)
    sigmoid_z = jax.nn.sigmoid(pre_act)
    factor = sigmoid_z * (1.0 + pre_act * (1.0 - sigmoid_z))
    dz = (grad_ref[...].astype(F32) * factor).astype(BF)
    back = lax.dot_general(
        dz, weight, (((1,), (1,)), ((), ())), preferred_element_type=F32
    ).astype(BF)
    for axis in (0, 1):
        backs[axis, 0, 0] = back[:, lanes[axis]]

    for i in (2, 1, 3):
        for axis in (0, 1):
            first[axis, i] = links.start(
                backs.at[axis, 0, 0], backs.at[axis, 0, i], beside(axis, i)
            )
    for w in (2, 1, 3):
        for axis in (0, 1):
            second[axis, w, 0] = links.start(
                backs.at[axis, 0, 0], backs.at[axis, w, 0], beside(1 - axis, w)
            )
    local_weight = lax.dot_general(
        agg, dz, (((0,), (0,)), ((), ())), preferred_element_type=F32
    )
    w_loc[...] = local_weight.astype(BF).reshape(w_loc.shape)
    w_first = {}
    for i in (2, 1, 3):
        to = lax.rem(x + i, SX)
        w_first[i] = links.start(w_loc.at[to], w_rx.at[i - 1], beside(0, i))
    for i in (1, 3, 2):
        for axis in (0, 1):
            first[axis, i].wait_recv()
    for w in (2, 1, 3):
        for axis in (0, 1):
            second[axis, w, 1] = links.start(
                backs.at[axis, 0, pl.ds(1, 3)],
                backs.at[axis, w, pl.ds(1, 3)],
                beside(1 - axis, w),
            )

    w_part = w_loc[x].astype(F32)
    for i in (1, 2, 3):
        w_first[i].wait_recv()
        w_part = w_part + w_rx[i - 1].astype(F32)
    w_sum[...] = w_part.astype(BF)
    w_second = {}
    for i in (2, 1, 3):
        to = lax.rem(y + i, SY)
        w_second[i] = links.start(w_sum.at[to], w_rx2.at[i - 1], beside(1, i))

    for axis in (0, 1):
        for w in (1, 3, 2):
            second[axis, w, 0].wait_recv()
            second[axis, w, 1].wait_recv()

    def back_tile_of(d):
        return lax.rem(x - d // SY + SX, SX) * SY + lax.rem(y - d % SY + SY, SY)

    def whole_back():
        left = [backs[0, d % SY, d // SY] for d in range(NCOL)]
        right = [backs[1, d // SY, d % SY] for d in range(NCOL)]
        return jnp.concatenate(
            [jnp.concatenate(left, axis=0), jnp.concatenate(right, axis=0)], axis=1
        )

    def transposed(columns):
        lhs = []
        for j in columns:
            lhs.append(
                jnp.concatenate(
                    [tiles_t[inv_s[back_tile_of(d), j]] for d in range(NCOL)], axis=1
                )
            )
        return jnp.dot(
            jnp.concatenate(lhs, axis=0),
            whole_back(),
            preferred_element_type=F32,
        )

    pair = {}

    def compute(offsets):
        for t0 in range(0, len(offsets), 2):
            some = offsets[t0 : t0 + 2]
            targets = [lax.rem(z + o + SZ, SZ) * 2 for o in some]
            terms = transposed(
                [t + 1 - core for t in targets] + [t + core for t in targets]
            )
            for n, o in enumerate(some):
                t = SLOT[o]
                pair_tx[t] = terms[n * tile : (n + 1) * tile].astype(BF)
                pair[t] = links.start(pair_tx.at[t], pair_rx.at[t], partner)
                m = n + len(some)
                own_t[t] = terms[m * tile : (m + 1) * tile]

    def pair_sum(o):
        t = SLOT[o]
        pair[t].wait_recv()
        return own_t[t] + pair_rx[t].astype(F32)

    leaf, chain = {}, {}

    def send_leaves(dist):
        for n, side in enumerate((1, -1)):
            m = dist // 2
            leaf_tx[n, m] = pair_sum(side * dist).astype(BF)
            leaf[side, dist] = links.start(
                leaf_tx.at[n, m], leaf_rx.at[n, m], at_z(side)
            )

    def send_chain(dist):
        m = dist // 2 - 1
        for n, side in enumerate((1, -1)):
            total = None if dist == 8 and n else pair_sum(side * dist)
            if total is None:
                total = eighth
            elif dist == 8:
                eighth = total
            else:
                leaf[side, dist + 1].wait_recv()
                total = total + leaf_rx[n, m + 1].astype(F32)
            for h in (n, 1 - n):
                at = pl.ds(h * half, half)
                mine = total[h * half : (h + 1) * half]
                if dist == 8 and h != n:
                    continue
                if dist < 6 or dist == 6 and h == n:
                    chain[side, dist + 2, h].wait_recv()
                    mine = mine + chain_rx[n, m + 1, at].astype(F32)
                chain_tx[n, m, at] = mine.astype(BF)
                chain[side, dist, h] = links.start(
                    chain_tx.at[n, m, at], chain_rx.at[n, m, at], at_z(2 * side)
                )

    compute([8, 7, -7])
    w_own = w_sum[y].astype(F32)
    for i in (1, 2, 3):
        w_second[i].wait_recv()
        w_own = w_own + w_rx2[i - 1].astype(F32)
    group, place = z // 4, z % 4
    w_far[group] = w_own.astype(BF)
    for i in (8, 4, -4):
        w_first[i] = links.start(w_far.at[group], w_far.at[group], at_z(i))
    compute([6, -6, 5, -5])
    send_chain(8)
    send_leaves(7)
    compute([4, -4, 3, -3])
    send_leaves(5)
    compute([2, -2, 1, -1])
    send_leaves(3)
    compute([0])
    send_chain(6)
    for i in (8, 4, -4):
        w_first[i].wait_recv()
    w_near[place] = jnp.sum(w_far[...].astype(F32), axis=0).astype(BF)
    for i in (2, 1, -1):
        w_second[i] = links.start(w_near.at[place], w_near.at[place], at_z(i))
    send_leaves(1)
    send_chain(4)
    for i in (2, 1, -1):
        w_second[i].wait_recv()
    w_pair[0] = jnp.sum(w_near[...].astype(F32), axis=0)
    w_cross = links.start(w_pair.at[0], w_pair.at[1], partner)
    w_cross.wait_recv()
    w_fin[x, y] = (w_pair[0] + w_pair[1]) * scaling
    for i in (2, 1, 3):
        w_first[i] = links.start(w_fin.at[x, y], w_fin.at[x, y], beside(1, i))
    send_chain(2)
    for i in (1, 3, 2):
        w_first[i].wait_recv()
    for i in (2, 1, 3):
        w_second[i] = links.start(w_fin.at[x], w_fin.at[x], beside(0, i))
    total = pair_sum(0)
    for n, side in enumerate((1, -1)):
        leaf[side, 1].wait_recv()
        total = total + leaf_rx[n, 0].astype(F32)
    for n, side in enumerate((1, -1)):
        for h in (n, 1 - n):
            chain[side, 2, h].wait_recv()
        total = total + chain_rx[n, 0].astype(F32)
    out_ref[...] = total.astype(BF)
    for i in (1, 3, 2):
        w_second[i].wait_recv()
    wout_ref[...] = w_fin[...].reshape(wout_ref.shape)
    links.drain()


PIECES = 2
COPIES = 192


def hand_out(a_ref, b_ref, c_ref, d_ref):
    c_ref[...] = a_ref[...]
    d_ref[...] = b_ref[...]


def body(features, weight, grad_out, tile_values, tile_coords, tile_count):
    tile, width = features.shape
    slots = tile_values.shape[2]
    nodes = tile * lax.axis_size("col") * lax.axis_size("row")
    vmem = pl.BlockSpec(memory_space=pltpu.VMEM)
    smem = pl.BlockSpec(memory_space=pltpu.SMEM)
    square = (tile, tile)
    slab = (tile, width)
    w_piece = (width // NCOL, width)
    done = pl.pallas_call(
        functools.partial(kernel, PIECES, 1.0 / math.sqrt(nodes)),
        out_shape=(
            jax.ShapeDtypeStruct(slab, BF),
            jax.ShapeDtypeStruct((width, width), F32),
        ),
        in_specs=[smem, vmem, vmem, vmem, vmem, pl.BlockSpec(memory_space=pl.ANY)],
        out_specs=(vmem, vmem),
        scratch_shapes=[
            pltpu.VMEM((16, 128), jnp.int32),
            pltpu.SMEM((16, 128), jnp.int32),
            pltpu.VMEM((slots + 1,) + square, BF),
            pltpu.VMEM((slots + 1,) + square, BF),
            pltpu.VMEM((16, 2) + slab, BF),
            pltpu.VMEM((NCOL * tile, width), F32),
            pltpu.VMEM((2, 4, 4) + square, BF),
            pltpu.VMEM((2, 4, 4) + square, BF),
            pltpu.VMEM((2, 4) + square, BF),
            pltpu.VMEM((2, 4) + square, BF),
            pltpu.VMEM((2, 4, 4) + square, BF),
            pltpu.VMEM((16,) + slab, F32),
            pltpu.VMEM((16,) + slab, BF),
            pltpu.VMEM((16,) + slab, BF),
            pltpu.VMEM((2, 4) + slab, BF),
            pltpu.VMEM((2, 4) + slab, BF),
            pltpu.VMEM((2, 4) + slab, BF),
            pltpu.VMEM((2, 4) + slab, BF),
            pltpu.VMEM((4, 4) + w_piece, BF),
            pltpu.VMEM((3, 4) + w_piece, BF),
            pltpu.VMEM((4,) + w_piece, BF),
            pltpu.VMEM((3,) + w_piece, BF),
            pltpu.VMEM((4,) + w_piece, BF),
            pltpu.VMEM((4,) + w_piece, BF),
            pltpu.VMEM((2,) + w_piece, F32),
            pltpu.VMEM((4, 4) + w_piece, F32),
            DMA((2,)),
            DMA((COPIES,)),
            DMA((COPIES,)),
        ],
        compiler_params=pltpu.CompilerParams(
            collective_id=0, has_side_effects=True, vmem_limit_bytes=56 << 20
        ),
        name="layer_backward",
    )(
        tile_coords[0, 0],
        tile_count,
        features,
        weight,
        grad_out,
        tile_values[0, 0],
    )
    return pl.pallas_call(
        hand_out,
        out_shape=tuple(jax.ShapeDtypeStruct(a.shape, a.dtype) for a in done),
        in_specs=[vmem, vmem],
        out_specs=(vmem, vmem),
        name="hand_out",
    )(*done)


def solution(mesh):
    return jax.shard_map(
        body,
        mesh=mesh,
        in_specs=(
            P(("col", "row"), None),
            P(),
            P(("col", "row"), None),
            P("col", "row", None, None, None),
            P("col", "row", None, None),
            P("col", "row"),
        ),
        out_specs=(P(("col", "row"), None), P()),
        check_vma=False,
    )
```

```python
import functools
import math

import jax
import jax.numpy as jnp
from jax import lax
from jax.experimental import pallas as pl
from jax.experimental.pallas import tpu as pltpu
from jax.sharding import PartitionSpec as P

MESH = pl.DeviceIdType.MESH
DMA = pltpu.SemaphoreType.DMA
BF = jnp.bfloat16
F32 = jnp.float32

SX, SY, SZ = 4, 4, 16
OFFS = (0, 1, -1, 2, -2, 3, -3, 4, -4, 5, -5, 6, -6, 7, -7, 8)
GROUPS = ((0, 1), (1, 5), (5, 9), (9, 13), (13, 16))
SLOT = {o: t for t, o in enumerate(OFFS)}
SLOT[-8] = SLOT[8]
NCOL = SX * SY


class Links:
    def __init__(self, send_sems, recv_sems):
        self.send_sems, self.recv_sems = send_sems, recv_sems
        self.used = 0
        self.sent = []

    def copy(self, src, dst, device):
        at = self.used
        self.used += 1
        return pltpu.make_async_remote_copy(
            src_ref=src,
            dst_ref=dst,
            send_sem=self.send_sems.at[at],
            recv_sem=self.recv_sems.at[at],
            device_id=device,
            device_id_type=MESH,
        )

    def start(self, src, dst, device):
        copy = self.copy(src, dst, device)
        copy.start()
        self.sent.append(copy)
        return copy

    def drain(self):
        for copy in self.sent:
            copy.wait_send()


def kernel(
    pieces,
    scaling,
    coords_ref,
    count_ref,
    feat_ref,
    weight_ref,
    grad_ref,
    tiles_ref,
    out_ref,
    wout_ref,
    coords_s,
    count_s,
    weight_v,
    grad_v,
    inv_v,
    inv_s,
    tiles,
    tiles_t,
    feats,
    acc,
    part,
    part_rx,
    sums,
    sums_rx,
    backs,
    own_t,
    pair_tx,
    pair_rx,
    leaf_tx,
    leaf_rx,
    chain_tx,
    chain_rx,
    w_loc,
    w_rx,
    w_far,
    w_near,
    w_fin,
    local_sems,
    send_sems,
    recv_sems,
):
    col, row = lax.axis_index("col"), lax.axis_index("row")
    x, y = col // SY, col % SY
    z, core = row // 2, row % 2
    links = Links(send_sems, recv_sems)
    slots = tiles_ref.shape[0]
    tile = tiles_ref.shape[1]
    half = tile // 2

    def at_z(offset):
        return (col, lax.rem(z + offset + SZ, SZ) * 2 + core)

    def across_z(offset):
        return (col, lax.rem(z + offset + SZ, SZ) * 2 + 1 - core)

    def col_at(dx, dy):
        return lax.rem(x + dx + SX, SX) * SY + lax.rem(y + dy + SY, SY)

    partner = (col, z * 2 + 1 - core)

    def beside(axis, offset):
        return (col_at(offset, 0) if axis == 0 else col_at(0, offset), row)

    barrier = pltpu.get_barrier_semaphore()
    greeted = [at_z(o) for o in (1, -1, 2, -2, 4, -4, 8)] + [partner]
    others = [(d // SY, d % SY) for d in range(NCOL - 1, 0, -1)]
    greeted += [(col_at(dx, dy), row) for dx, dy in others]
    greeted += [across_z(o) for o in (1, -1, 2, -2)]
    for device in greeted:
        pl.semaphore_signal(barrier, inc=1, device_id=device, device_id_type=MESH)

    def load(n, src, dst):
        copy = pltpu.make_async_copy(src, dst, local_sems.at[n])
        copy.start()
        return copy

    load_coords = load(0, coords_ref, coords_s)
    load_count = load(1, count_ref, count_s)
    load_feats = load(2, feat_ref, feats.at[0, 0])
    load_tiles = load(3, tiles_ref, tiles.at[pl.ds(1, slots)])
    load_weight = load(4, weight_ref, weight_v)
    load_grad = load(5, grad_ref, grad_v)

    tile_row = lax.broadcasted_iota(jnp.int32, inv_v.shape, 0)
    tile_col = lax.broadcasted_iota(jnp.int32, inv_v.shape, 1)
    load_coords.wait()
    load_count.wait()
    live = count_s[0, 0]

    def enter(k, table):
        hit = (tile_row == coords_s[0, k]) & (tile_col == coords_s[1, k])
        hit = hit & (jnp.full(inv_v.shape, k, jnp.int32) < live)
        return jnp.where(hit, k + 1, table)

    inv_v[...] = lax.fori_loop(
        0, slots, enter, jnp.zeros(inv_v.shape, jnp.int32), unroll=8
    )
    table_copy = pltpu.make_async_copy(inv_v, inv_s, local_sems.at[6])
    table_copy.start()
    load_feats.wait()
    pl.semaphore_wait(barrier, len(greeted))

    ahead = {}
    rows_of = tile // pieces

    def rows(p):
        return pl.ds(p * rows_of, rows_of)

    def feat_at(t, p):
        return feats.at[t, 0, rows(p)]

    def stride(dist):
        for p in range(pieces):
            for side in (1, -1):
                far = dist + 2
                if dist:
                    ahead[side * dist, p].wait_recv()
                if far == 8 and (p < pieces // 2) != (side == 1):
                    continue
                ahead[side * far, p] = links.start(
                    feat_at(SLOT[side * dist], p),
                    feat_at(SLOT[side * far], p),
                    at_z(side * 2),
                )

    def hand_over(dist):
        for side in (1, -1):
            ahead[side * (dist + 1)] = links.start(
                feats.at[SLOT[side * dist], 0],
                feats.at[SLOT[side * (dist + 1)], 0],
                at_z(side),
            )

    crossed = {}

    def cross(t):
        crossed[t] = links.start(feats.at[t, 0], feats.at[t, 1], partner)

    stride(0)
    hand_over(0)
    cross(0)

    tiles[0] = jnp.zeros(tiles.shape[1:], BF)
    tiles_t[0] = jnp.zeros(tiles.shape[1:], BF)
    table_copy.wait()
    load_tiles.wait()

    def column_tile(t, other):
        source = lax.rem(z - OFFS[t] + SZ, SZ)
        return source * 2 + (1 - core if other else core)

    block = 4

    order = [
        (a + i, b + j) for a, b in ((2, 2), (2, 0), (0, 2), (0, 0)) for i in (0, 1) for j in (0, 1)
    ]

    def row_tile_of(q):
        a = 2 - 2 * (q // 8) + q % 4 // 2
        b = 2 - 2 * (q // 4 % 2) + q % 2
        return lax.rem(x + a, SX) * SY + lax.rem(y + b, SY)

    def product(lo, hi, q0):
        columns = [column_tile(t, o) for t in range(lo, hi) for o in (0, 1)]
        lhs = []
        for a in range(block):
            i = row_tile_of(q0 + a)
            lhs.append(jnp.concatenate([tiles[inv_s[i, j]] for j in columns], axis=1))
        rhs = feats[lo:hi].reshape((hi - lo) * 2 * tile, -1)
        return jnp.dot(
            jnp.concatenate(lhs, axis=0), rhs, preferred_element_type=F32
        )

    def accumulate(lo, hi):
        def one(b, carry):
            at = pl.ds(pl.multiple_of(b * block * tile, block * tile), block * tile)
            if lo == 0:
                acc[at] = product(lo, hi, b * block)
            else:
                acc[at] += product(lo, hi, b * block)
            return carry

        lax.fori_loop(0, NCOL // block, one, 0)

    def flip(k, carry):
        tiles_t[k + 1] = tiles[k + 1].T
        return carry

    lax.fori_loop(0, slots, flip, 0, unroll=4)
    for s in range(1, 5):
        if s < 4:
            stride(2 * s)
            hand_over(2 * s)
        else:
            for p in range(pieces):
                ahead[8 if p < pieces // 2 else -8, p].wait_recv()
        for side in (1, -1):
            if s < 4:
                cross(SLOT[side * 2 * s])
            ahead[side * (2 * s - 1)].wait_recv()
            cross(SLOT[side * (2 * s - 1)])
        if s == 4:
            cross(SLOT[8])
        lo, hi = GROUPS[s - 1]
        for t in range(lo, hi):
            crossed[t].wait_recv()
        accumulate(lo, hi)

    lo, hi = GROUPS[-1]
    for t in range(lo, hi):
        crossed[t].wait_recv()

    lanes = [slice(0, 128), slice(128, 256)]
    first = {}
    for b in range(NCOL // block):
        at = pl.ds(b * block * tile, block * tile)
        total = (acc[at] + product(lo, hi, b * block)).astype(BF)
        some = order[b * block : (b + 1) * block]
        for n, (dx, dy) in enumerate(some):
            for axis, (i, w) in enumerate(((dx, dy), (dy, dx))):
                part[axis, i, w] = total[n * tile : (n + 1) * tile, lanes[axis]]
        for axis in (0, 1):
            for i in sorted({d[axis] for d in some}):
                w = min(d[1 - axis] for d in some)
                if i:
                    first[axis, i, w] = links.start(
                        part.at[axis, i, pl.ds(w, 2)],
                        part_rx.at[axis, i, pl.ds(w, 2)],
                        beside(axis, i),
                    )
    second = {}
    own_sum = {}
    for w0 in (2, 0):
        for axis in (0, 1):
            for i in (1, 2, 3):
                first[axis, i, w0].wait_recv()
            for w in (w0 + 1, w0) if w0 == 0 else (w0, w0 + 1):
                mine = part[axis, 0, w].astype(F32)
                for i in (1, 2, 3):
                    mine = mine + part_rx[axis, i, w].astype(F32)
                if w:
                    sums[axis, w] = mine.astype(BF)
                    second[axis, w] = links.start(
                        sums.at[axis, w], sums_rx.at[axis, w], beside(1 - axis, w)
                    )
                else:
                    own_sum[axis] = mine
    halves = []
    for axis in (0, 1):
        mine = own_sum[axis]
        for w in (2, 3, 1):
            second[axis, w].wait_recv()
            mine = mine + sums_rx[axis, w].astype(F32)
        halves.append(mine)
    agg = jnp.concatenate(halves, axis=1)
    agg = agg.astype(BF)

    load_weight.wait()
    load_grad.wait()
    weight = weight_v[...]
    pre_act = jnp.dot(agg, weight, preferred_element_type=F32)
    sigmoid_z = jax.nn.sigmoid(pre_act)
    factor = sigmoid_z * (1.0 + pre_act * (1.0 - sigmoid_z))
    dz = (grad_v[...].astype(F32) * factor).astype(BF)
    back = lax.dot_general(
        dz, weight, (((1,), (1,)), ((), ())), preferred_element_type=F32
    ).astype(BF)
    for axis in (0, 1):
        backs[axis, 0, 0] = back[:, lanes[axis]]

    for i in (2, 1, 3):
        for axis in (0, 1):
            first[axis, i] = links.start(
                backs.at[axis, 0, 0], backs.at[axis, 0, i], beside(axis, i)
            )
    for w in (2, 1, 3):
        for axis in (0, 1):
            second[axis, w, 0] = links.start(
                backs.at[axis, 0, 0], backs.at[axis, w, 0], beside(1 - axis, w)
            )
    local_weight = lax.dot_general(
        agg, dz, (((0,), (0,)), ((), ())), preferred_element_type=F32
    )
    w_loc[...] = local_weight.astype(BF).reshape(w_loc.shape)
    w_copies = {}
    for n, (dx, dy) in enumerate(others):
        to = (lax.rem(x + dx, SX), lax.rem(y + dy, SY))
        w_copies[n] = links.start(
            w_loc.at[to[0], to[1]], w_rx.at[n], (col_at(dx, dy), row)
        )
    for i in (1, 3, 2):
        for axis in (0, 1):
            first[axis, i].wait_recv()
    for w in (2, 1, 3):
        for axis in (0, 1):
            second[axis, w, 1] = links.start(
                backs.at[axis, 0, pl.ds(1, 3)],
                backs.at[axis, w, pl.ds(1, 3)],
                beside(1 - axis, w),
            )

    w_own = w_loc[x, y].astype(F32)
    for n in range(len(others)):
        w_copies[n].wait_recv()
        w_own = w_own + w_rx[n].astype(F32)
    group, place = z // 4, z % 4
    w_far[group] = w_own.astype(BF)
    for i in (8, 4, -4):
        w_copies[i] = links.start(w_far.at[group], w_far.at[group], at_z(i))

    for axis in (0, 1):
        for w in (1, 3, 2):
            second[axis, w, 0].wait_recv()
            second[axis, w, 1].wait_recv()

    def back_tile_of(d):
        return lax.rem(x - d // SY + SX, SX) * SY + lax.rem(y - d % SY + SY, SY)

    def whole_back():
        left = [backs[0, d % SY, d // SY] for d in range(NCOL)]
        right = [backs[1, d // SY, d % SY] for d in range(NCOL)]
        return jnp.concatenate(
            [jnp.concatenate(left, axis=0), jnp.concatenate(right, axis=0)], axis=1
        )

    def transposed(columns):
        lhs = []
        for j in columns:
            lhs.append(
                jnp.concatenate(
                    [tiles_t[inv_s[back_tile_of(d), j]] for d in range(NCOL)], axis=1
                )
            )
        return jnp.dot(
            jnp.concatenate(lhs, axis=0),
            whole_back(),
            preferred_element_type=F32,
        )

    pair = {}

    def compute(offsets):
        for t0 in range(0, len(offsets), 2):
            some = offsets[t0 : t0 + 2]
            targets = [lax.rem(z + o + SZ, SZ) * 2 for o in some]
            terms = transposed(
                [t + 1 - core for t in targets] + [t + core for t in targets]
            )
            for n, o in enumerate(some):
                t = SLOT[o]
                pair_tx[t] = terms[n * tile : (n + 1) * tile].astype(BF)
                pair[t] = links.start(pair_tx.at[t], pair_rx.at[t], partner)
                m = n + len(some)
                own_t[t] = terms[m * tile : (m + 1) * tile]

    def pair_sum(o):
        t = SLOT[o]
        pair[t].wait_recv()
        return own_t[t] + pair_rx[t].astype(F32)

    leaf, chain = {}, {}

    def send_leaves(dist):
        for n, side in enumerate((1, -1)):
            m = dist // 2
            leaf_tx[n, m] = pair_sum(side * dist).astype(BF)
            leaf[side, dist] = links.start(
                leaf_tx.at[n, m], leaf_rx.at[n, m], at_z(side)
            )

    def send_chain(dist):
        m = dist // 2 - 1
        totals = []
        for n, side in enumerate((1, -1)):
            if dist == 8:
                totals.append(totals[0] if n else pair_sum(8))
            else:
                total = pair_sum(side * dist)
                leaf[side, dist + 1].wait_recv()
                totals.append(total + leaf_rx[n, m + 1].astype(F32))
        for turn in range(1 if dist == 8 else 2):
            for n, side in enumerate((1, -1)):
                h = (n + turn) % 2
                at = pl.ds(h * half, half)
                mine = totals[n][h * half : (h + 1) * half]
                if dist < 6 or dist == 6 and turn == 0:
                    chain[side, dist + 2, h].wait_recv()
                    mine = mine + chain_rx[n, m + 1, at].astype(F32)
                chain_tx[n, m, at] = mine.astype(BF)
                chain[side, dist, h] = links.start(
                    chain_tx.at[n, m, at], chain_rx.at[n, m, at], at_z(2 * side)
                )

    compute([8])
    compute([7, -7])
    send_chain(8)
    compute([6, -6])
    send_leaves(7)
    compute([5, -5])
    compute([4, -4])
    send_leaves(5)
    compute([3, -3])
    send_chain(6)
    send_leaves(3)
    for i in (8, 4, -4):
        w_copies[i].wait_recv()
    mine = place * 2 + core
    w_near[mine] = jnp.sum(w_far[...].astype(F32), axis=0).astype(BF)
    for n, device in enumerate(
        [f(o) for o in (2, 1, -1) for f in (at_z, across_z)] + [partner]
    ):
        w_copies[n] = links.start(w_near.at[mine], w_near.at[mine], device)
    compute([2, -2])
    compute([1, -1])
    compute([0])
    send_leaves(1)
    send_chain(4)
    for n in range(7):
        w_copies[n].wait_recv()
    w_fin[x, y] = (jnp.sum(w_near[...].astype(F32), axis=0) * scaling).astype(BF)
    for n, (dx, dy) in enumerate(others):
        w_copies[n] = links.start(
            w_fin.at[x, y], w_fin.at[x, y], (col_at(dx, dy), row)
        )
    send_chain(2)
    total = pair_sum(0)
    for n, side in enumerate((1, -1)):
        leaf[side, 1].wait_recv()
        total = total + leaf_rx[n, 0].astype(F32)
    for n, side in enumerate((1, -1)):
        for h in (n, 1 - n):
            chain[side, 2, h].wait_recv()
        total = total + chain_rx[n, 0].astype(F32)
    out_ref[...] = total.astype(BF)
    for n in range(len(others)):
        w_copies[n].wait_recv()
    wout_ref[...] = w_fin[...].astype(F32).reshape(wout_ref.shape)
    links.drain()


PIECES = 2
COPIES = 192


def hand_out(a_ref, b_ref, c_ref, d_ref):
    c_ref[...] = a_ref[...]
    d_ref[...] = b_ref[...]


def body(features, weight, grad_out, tile_values, tile_coords, tile_count):
    tile, width = features.shape
    slots = tile_values.shape[2]
    nodes = tile * lax.axis_size("col") * lax.axis_size("row")
    vmem = pl.BlockSpec(memory_space=pltpu.VMEM)
    square = (tile, tile)
    slab = (tile, width)
    w_piece = (width // NCOL, width)
    done = pl.pallas_call(
        functools.partial(kernel, PIECES, 1.0 / math.sqrt(nodes)),
        out_shape=(
            jax.ShapeDtypeStruct(slab, BF),
            jax.ShapeDtypeStruct((width, width), F32),
        ),
        in_specs=[pl.BlockSpec(memory_space=pltpu.HBM)] * 6,
        out_specs=(vmem, vmem),
        scratch_shapes=[
            pltpu.SMEM((2, slots), jnp.int32),
            pltpu.SMEM((1, 1), jnp.int32),
            pltpu.VMEM((width, width), BF),
            pltpu.VMEM(slab, BF),
            pltpu.VMEM((16, 128), jnp.int32),
            pltpu.SMEM((16, 128), jnp.int32),
            pltpu.VMEM((slots + 1,) + square, BF),
            pltpu.VMEM((slots + 1,) + square, BF),
            pltpu.VMEM((16, 2) + slab, BF),
            pltpu.VMEM((NCOL * tile, width), F32),
            pltpu.VMEM((2, 4, 4) + square, BF),
            pltpu.VMEM((2, 4, 4) + square, BF),
            pltpu.VMEM((2, 4) + square, BF),
            pltpu.VMEM((2, 4) + square, BF),
            pltpu.VMEM((2, 4, 4) + square, BF),
            pltpu.VMEM((16,) + slab, F32),
            pltpu.VMEM((16,) + slab, BF),
            pltpu.VMEM((16,) + slab, BF),
            pltpu.VMEM((2, 4) + slab, BF),
            pltpu.VMEM((2, 4) + slab, BF),
            pltpu.VMEM((2, 4) + slab, BF),
            pltpu.VMEM((2, 4) + slab, BF),
            pltpu.VMEM((4, 4) + w_piece, BF),
            pltpu.VMEM((NCOL - 1,) + w_piece, BF),
            pltpu.VMEM((4,) + w_piece, BF),
            pltpu.VMEM((8,) + w_piece, BF),
            pltpu.VMEM((4, 4) + w_piece, BF),
            DMA((7,)),
            DMA((COPIES,)),
            DMA((COPIES,)),
        ],
        compiler_params=pltpu.CompilerParams(
            collective_id=0, has_side_effects=True, vmem_limit_bytes=56 << 20
        ),
        name="layer_backward",
    )(
        tile_coords[0, 0],
        tile_count,
        features,
        weight,
        grad_out,
        tile_values[0, 0],
    )
    return pl.pallas_call(
        hand_out,
        out_shape=tuple(jax.ShapeDtypeStruct(a.shape, a.dtype) for a in done),
        in_specs=[vmem, vmem],
        out_specs=(vmem, vmem),
        name="hand_out",
    )(*done)


def solution(mesh):
    return jax.shard_map(
        body,
        mesh=mesh,
        in_specs=(
            P(("col", "row"), None),
            P(),
            P(("col", "row"), None),
            P("col", "row", None, None, None),
            P("col", "row", None, None),
            P("col", "row"),
        ),
        out_specs=(P(("col", "row"), None), P()),
        check_vma=False,
    )
```

```python
import functools
import math

import jax
import jax.numpy as jnp
from jax import lax
from jax.experimental import pallas as pl
from jax.experimental.pallas import tpu as pltpu
from jax.sharding import PartitionSpec as P

MESH = pl.DeviceIdType.MESH
DMA = pltpu.SemaphoreType.DMA
BF = jnp.bfloat16
F32 = jnp.float32

SX, SY, SZ = 4, 4, 16
OFFS = (0, 1, -1, 2, -2, 3, -3, 4, -4, 5, -5, 6, -6, 7, -7, 8)
GROUPS = ((0, 1), (1, 5), (5, 9), (9, 13), (13, 16))
SLOT = {o: t for t, o in enumerate(OFFS)}
SLOT[-8] = SLOT[8]
NCOL = SX * SY


class Links:
    def __init__(self, send_sems, recv_sems):
        self.send_sems, self.recv_sems = send_sems, recv_sems
        self.used = 0
        self.sent = []

    def copy(self, src, dst, device):
        at = self.used
        self.used += 1
        return pltpu.make_async_remote_copy(
            src_ref=src,
            dst_ref=dst,
            send_sem=self.send_sems.at[at],
            recv_sem=self.recv_sems.at[at],
            device_id=device,
            device_id_type=MESH,
        )

    def start(self, src, dst, device):
        copy = self.copy(src, dst, device)
        copy.start()
        self.sent.append(copy)
        return copy

    def drain(self, keep=0):
        cut = len(self.sent) - keep
        for copy in self.sent[:cut]:
            copy.wait_send()
        self.sent = self.sent[cut:]


def kernel(
    pieces,
    chain_pieces,
    scaling,
    coords_ref,
    count_ref,
    feat_ref,
    weight_ref,
    grad_ref,
    tiles_ref,
    out_ref,
    wout_ref,
    coords_s,
    count_s,
    weight_v,
    grad_v,
    inv_v,
    inv_s,
    tiles,
    tiles_t,
    feats,
    acc,
    part,
    part_rx,
    sums,
    sums_rx,
    backs,
    own_t,
    pair_tx,
    pair_rx,
    leaf_tx,
    leaf_rx,
    chain_tx,
    chain_rx,
    w_loc,
    w_rx,
    w_far,
    w_near,
    w_fin,
    local_sems,
    send_sems,
    recv_sems,
):
    col, row = lax.axis_index("col"), lax.axis_index("row")
    x, y = col // SY, col % SY
    z, core = row // 2, row % 2
    links = Links(send_sems, recv_sems)
    slots = tiles_ref.shape[0]
    tile = tiles_ref.shape[1]
    chain_rows = tile // chain_pieces

    def at_z(offset):
        return (col, lax.rem(z + offset + SZ, SZ) * 2 + core)

    def across_z(offset):
        return (col, lax.rem(z + offset + SZ, SZ) * 2 + 1 - core)

    def col_at(dx, dy):
        return lax.rem(x + dx + SX, SX) * SY + lax.rem(y + dy + SY, SY)

    partner = (col, z * 2 + 1 - core)

    def beside(axis, offset):
        return (col_at(offset, 0) if axis == 0 else col_at(0, offset), row)

    barrier = pltpu.get_barrier_semaphore()
    greeted = [at_z(o) for o in (1, -1, 2, -2, 4, -4, 8)] + [partner]
    others = [(d // SY, d % SY) for d in range(NCOL - 1, 0, -1)]
    greeted += [(col_at(dx, dy), row) for dx, dy in others]
    greeted += [across_z(o) for o in (1, -1, 2, -2)]
    for device in greeted:
        pl.semaphore_signal(barrier, inc=1, device_id=device, device_id_type=MESH)

    def load(n, src, dst):
        copy = pltpu.make_async_copy(src, dst, local_sems.at[n])
        copy.start()
        return copy

    load_coords = load(0, coords_ref, coords_s)
    load_count = load(1, count_ref, count_s)
    load_feats = load(2, feat_ref, feats.at[0, 0])
    load_tiles = load(3, tiles_ref, tiles.at[pl.ds(1, slots)])
    load_weight = load(4, weight_ref, weight_v)
    load_grad = load(5, grad_ref, grad_v)

    tile_row = lax.broadcasted_iota(jnp.int32, inv_v.shape, 0)
    tile_col = lax.broadcasted_iota(jnp.int32, inv_v.shape, 1)
    load_coords.wait()
    load_count.wait()
    live = count_s[0, 0]

    def enter(k, table):
        hit = (tile_row == coords_s[0, k]) & (tile_col == coords_s[1, k])
        hit = hit & (jnp.full(inv_v.shape, k, jnp.int32) < live)
        return jnp.where(hit, k + 1, table)

    inv_v[...] = lax.fori_loop(
        0, slots, enter, jnp.zeros(inv_v.shape, jnp.int32), unroll=8
    )
    table_copy = pltpu.make_async_copy(inv_v, inv_s, local_sems.at[6])
    table_copy.start()
    load_feats.wait()
    pl.semaphore_wait(barrier, len(greeted))

    ahead = {}
    rows_of = tile // pieces

    def rows(p):
        return pl.ds(p * rows_of, rows_of)

    def feat_at(t, p):
        return feats.at[t, 0, rows(p)]

    def stride(dist):
        for p in range(pieces):
            for side in (1, -1):
                far = dist + 2
                if dist:
                    ahead[side * dist, p].wait_recv()
                if far == 8 and (p < pieces // 2) != (side == 1):
                    continue
                ahead[side * far, p] = links.start(
                    feat_at(SLOT[side * dist], p),
                    feat_at(SLOT[side * far], p),
                    at_z(side * 2),
                )

    def hand_over(dist):
        for side in (1, -1):
            ahead[side * (dist + 1)] = links.start(
                feats.at[SLOT[side * dist], 0],
                feats.at[SLOT[side * (dist + 1)], 0],
                at_z(side),
            )

    crossed = {}

    def cross(t):
        crossed[t] = links.start(feats.at[t, 0], feats.at[t, 1], partner)

    stride(0)
    hand_over(0)
    cross(0)

    tiles[0] = jnp.zeros(tiles.shape[1:], BF)
    tiles_t[0] = jnp.zeros(tiles.shape[1:], BF)
    table_copy.wait()
    load_tiles.wait()

    def column_tile(t, other):
        source = lax.rem(z - OFFS[t] + SZ, SZ)
        return source * 2 + (1 - core if other else core)

    block = 4

    order = [
        (a + i, b + j) for a, b in ((2, 2), (2, 0), (0, 2), (0, 0)) for i in (0, 1) for j in (0, 1)
    ]

    def row_tile_of(q):
        a = 2 - 2 * (q // 8) + q % 4 // 2
        b = 2 - 2 * (q // 4 % 2) + q % 2
        return lax.rem(x + a, SX) * SY + lax.rem(y + b, SY)

    def product(lo, hi, q0):
        columns = [column_tile(t, o) for t in range(lo, hi) for o in (0, 1)]
        lhs = []
        for a in range(block):
            i = row_tile_of(q0 + a)
            lhs.append(jnp.concatenate([tiles[inv_s[i, j]] for j in columns], axis=1))
        rhs = feats[lo:hi].reshape((hi - lo) * 2 * tile, -1)
        return jnp.dot(
            jnp.concatenate(lhs, axis=0), rhs, preferred_element_type=F32
        )

    def accumulate(lo, hi):
        def one(b, carry):
            at = pl.ds(pl.multiple_of(b * block * tile, block * tile), block * tile)
            if lo == 0:
                acc[at] = product(lo, hi, b * block)
            else:
                acc[at] += product(lo, hi, b * block)
            return carry

        lax.fori_loop(0, NCOL // block, one, 0)

    def flip(k, carry):
        tiles_t[k + 1] = tiles[k + 1].T
        return carry

    lax.fori_loop(0, slots, flip, 0, unroll=4)
    for s in range(1, 5):
        if s < 4:
            stride(2 * s)
            hand_over(2 * s)
        else:
            for p in range(pieces):
                ahead[8 if p < pieces // 2 else -8, p].wait_recv()
        for side in (1, -1):
            if s < 4:
                cross(SLOT[side * 2 * s])
            ahead[side * (2 * s - 1)].wait_recv()
            cross(SLOT[side * (2 * s - 1)])
        if s == 4:
            cross(SLOT[8])
        lo, hi = GROUPS[s - 1]
        for t in range(lo, hi):
            crossed[t].wait_recv()
        accumulate(lo, hi)

    lo, hi = GROUPS[-1]
    for t in range(lo, hi):
        crossed[t].wait_recv()

    lanes = [slice(0, 128), slice(128, 256)]
    first = {}
    for b in range(NCOL // block):
        at = pl.ds(b * block * tile, block * tile)
        total = (acc[at] + product(lo, hi, b * block)).astype(BF)
        some = order[b * block : (b + 1) * block]
        for n, (dx, dy) in enumerate(some):
            for axis, (i, w) in enumerate(((dx, dy), (dy, dx))):
                part[axis, i, w] = total[n * tile : (n + 1) * tile, lanes[axis]]
        for axis in (0, 1):
            for i in sorted({d[axis] for d in some}):
                w = min(d[1 - axis] for d in some)
                if i:
                    first[axis, i, w] = links.start(
                        part.at[axis, i, pl.ds(w, 2)],
                        part_rx.at[axis, i, pl.ds(w, 2)],
                        beside(axis, i),
                    )
    links.drain(12)
    second = {}
    own_sum = {}
    for w0 in (2, 0):
        for axis in (0, 1):
            for i in (1, 2, 3):
                first[axis, i, w0].wait_recv()
            for w in (w0 + 1, w0) if w0 == 0 else (w0, w0 + 1):
                mine = part[axis, 0, w].astype(F32)
                for i in (1, 2, 3):
                    mine = mine + part_rx[axis, i, w].astype(F32)
                if w:
                    sums[axis, w] = mine.astype(BF)
                    second[axis, w] = links.start(
                        sums.at[axis, w], sums_rx.at[axis, w], beside(1 - axis, w)
                    )
                else:
                    own_sum[axis] = mine
    halves = []
    for axis in (0, 1):
        mine = own_sum[axis]
        for w in (2, 3, 1):
            second[axis, w].wait_recv()
            mine = mine + sums_rx[axis, w].astype(F32)
        halves.append(mine)
    agg = jnp.concatenate(halves, axis=1)
    agg = agg.astype(BF)

    load_weight.wait()
    load_grad.wait()
    weight = weight_v[...]
    pre_act = jnp.dot(agg, weight, preferred_element_type=F32)
    sigmoid_z = jax.nn.sigmoid(pre_act)
    factor = sigmoid_z * (1.0 + pre_act * (1.0 - sigmoid_z))
    dz = (grad_v[...].astype(F32) * factor).astype(BF)
    back = lax.dot_general(
        dz, weight, (((1,), (1,)), ((), ())), preferred_element_type=F32
    ).astype(BF)
    for axis in (0, 1):
        backs[axis, 0, 0] = back[:, lanes[axis]]

    for i in (2, 1, 3):
        for axis in (0, 1):
            first[axis, i] = links.start(
                backs.at[axis, 0, 0], backs.at[axis, 0, i], beside(axis, i)
            )
    for w in (2, 1, 3):
        for axis in (0, 1):
            second[axis, w, 0] = links.start(
                backs.at[axis, 0, 0], backs.at[axis, w, 0], beside(1 - axis, w)
            )
    local_weight = lax.dot_general(
        agg, dz, (((0,), (0,)), ((), ())), preferred_element_type=F32
    )
    w_loc[...] = local_weight.astype(BF).reshape(w_loc.shape)
    w_copies = {}
    for n, (dx, dy) in enumerate(others):
        to = (lax.rem(x + dx, SX), lax.rem(y + dy, SY))
        w_copies[n] = links.start(
            w_loc.at[to[0], to[1]], w_rx.at[n], (col_at(dx, dy), row)
        )
    links.drain(27)
    for i in (1, 3, 2):
        for axis in (0, 1):
            first[axis, i].wait_recv()
    for w in (2, 1, 3):
        for axis in (0, 1):
            second[axis, w, 1] = links.start(
                backs.at[axis, 0, pl.ds(1, 3)],
                backs.at[axis, w, pl.ds(1, 3)],
                beside(1 - axis, w),
            )

    w_own = w_loc[x, y].astype(F32)
    for n in range(len(others)):
        w_copies[n].wait_recv()
        w_own = w_own + w_rx[n].astype(F32)
    group, place = z // 4, z % 4
    w_far[group] = w_own.astype(BF)
    for i in (8, 4, -4):
        w_copies[i] = links.start(w_far.at[group], w_far.at[group], at_z(i))

    links.drain(9)
    for axis in (0, 1):
        for w in (1, 3, 2):
            second[axis, w, 0].wait_recv()
            second[axis, w, 1].wait_recv()

    def back_tile_of(d):
        return lax.rem(x - d // SY + SX, SX) * SY + lax.rem(y - d % SY + SY, SY)

    def whole_back():
        left = [backs[0, d % SY, d // SY] for d in range(NCOL)]
        right = [backs[1, d // SY, d % SY] for d in range(NCOL)]
        return jnp.concatenate(
            [jnp.concatenate(left, axis=0), jnp.concatenate(right, axis=0)], axis=1
        )

    def transposed(columns):
        lhs = []
        for j in columns:
            lhs.append(
                jnp.concatenate(
                    [tiles_t[inv_s[back_tile_of(d), j]] for d in range(NCOL)], axis=1
                )
            )
        return jnp.dot(
            jnp.concatenate(lhs, axis=0),
            whole_back(),
            preferred_element_type=F32,
        )

    pair = {}

    def compute(offsets):
        for t0 in range(0, len(offsets), 2):
            some = offsets[t0 : t0 + 2]
            targets = [lax.rem(z + o + SZ, SZ) * 2 for o in some]
            terms = transposed(
                [t + 1 - core for t in targets] + [t + core for t in targets]
            )
            for n, o in enumerate(some):
                t = SLOT[o]
                pair_tx[t] = terms[n * tile : (n + 1) * tile].astype(BF)
                pair[t] = links.start(pair_tx.at[t], pair_rx.at[t], partner)
                m = n + len(some)
                own_t[t] = terms[m * tile : (m + 1) * tile]

    def pair_sum(o):
        t = SLOT[o]
        pair[t].wait_recv()
        return own_t[t] + pair_rx[t].astype(F32)

    leaf, chain = {}, {}

    def send_leaves(dist):
        for n, side in enumerate((1, -1)):
            m = dist // 2
            leaf_tx[n, m] = pair_sum(side * dist).astype(BF)
            leaf[side, dist] = links.start(
                leaf_tx.at[n, m], leaf_rx.at[n, m], at_z(side)
            )

    def send_chain(dist):
        m = dist // 2 - 1
        totals = []
        for n, side in enumerate((1, -1)):
            if dist == 8:
                totals.append(totals[0] if n else pair_sum(8))
            else:
                total = pair_sum(side * dist)
                leaf[side, dist + 1].wait_recv()
                totals.append(total + leaf_rx[n, m + 1].astype(F32))
        apart = chain_pieces // 2
        for turn in range(apart if dist == 8 else chain_pieces):
            for n, side in enumerate((1, -1)):
                h = (n * apart + turn) % chain_pieces
                at = pl.ds(h * chain_rows, chain_rows)
                mine = totals[n][h * chain_rows : (h + 1) * chain_rows]
                if dist < 6 or dist == 6 and turn < apart:
                    chain[side, dist + 2, h].wait_recv()
                    mine = mine + chain_rx[n, m + 1, at].astype(F32)
                chain_tx[n, m, at] = mine.astype(BF)
                chain[side, dist, h] = links.start(
                    chain_tx.at[n, m, at], chain_rx.at[n, m, at], at_z(2 * side)
                )

    compute([8])
    compute([7, -7])
    send_chain(8)
    compute([6, -6])
    send_leaves(7)
    compute([5, -5])
    compute([4, -4])
    send_leaves(5)
    compute([3, -3])
    send_chain(6)
    send_leaves(3)
    for i in (8, 4, -4):
        w_copies[i].wait_recv()
    mine = place * 2 + core
    w_near[mine] = jnp.sum(w_far[...].astype(F32), axis=0).astype(BF)
    for n, device in enumerate(
        [f(o) for o in (2, 1, -1) for f in (at_z, across_z)] + [partner]
    ):
        w_copies[n] = links.start(w_near.at[mine], w_near.at[mine], device)
    compute([2, -2])
    compute([1, -1])
    compute([0])
    send_leaves(1)
    links.drain(20)
    send_chain(4)
    for n in range(7):
        w_copies[n].wait_recv()
    w_fin[x, y] = (jnp.sum(w_near[...].astype(F32), axis=0) * scaling).astype(BF)
    for n, (dx, dy) in enumerate(others):
        w_copies[n] = links.start(
            w_fin.at[x, y], w_fin.at[x, y], (col_at(dx, dy), row)
        )
    links.drain(15 + 2 * chain_pieces)
    send_chain(2)
    links.drain(2 * chain_pieces)
    total = pair_sum(0)
    for n, side in enumerate((1, -1)):
        leaf[side, 1].wait_recv()
        total = total + leaf_rx[n, 0].astype(F32)
    for n, side in enumerate((1, -1)):
        for h in range(chain_pieces):
            chain[side, 2, h].wait_recv()
        total = total + chain_rx[n, 0].astype(F32)
    out_ref[...] = total.astype(BF)
    for n in range(len(others)):
        w_copies[n].wait_recv()
    wout_ref[...] = w_fin[...].astype(F32).reshape(wout_ref.shape)
    links.drain()


PIECES = 4
CHAIN_PIECES = 2
COPIES = 192


def body(features, weight, grad_out, tile_values, tile_coords, tile_count):
    tile, width = features.shape
    slots = tile_values.shape[2]
    nodes = tile * lax.axis_size("col") * lax.axis_size("row")
    vmem = pl.BlockSpec(memory_space=pltpu.VMEM)
    square = (tile, tile)
    slab = (tile, width)
    w_piece = (width // NCOL, width)
    return pl.pallas_call(
        functools.partial(kernel, PIECES, CHAIN_PIECES, 1.0 / math.sqrt(nodes)),
        out_shape=(pltpu.VMEM(slab, BF), pltpu.VMEM((width, width), F32)),
        in_specs=[pl.BlockSpec(memory_space=pltpu.HBM)] * 6,
        out_specs=(vmem, vmem),
        scratch_shapes=[
            pltpu.SMEM((2, slots), jnp.int32),
            pltpu.SMEM((1, 1), jnp.int32),
            pltpu.VMEM((width, width), BF),
            pltpu.VMEM(slab, BF),
            pltpu.VMEM((16, 128), jnp.int32),
            pltpu.SMEM((16, 128), jnp.int32),
            pltpu.VMEM((slots + 1,) + square, BF),
            pltpu.VMEM((slots + 1,) + square, BF),
            pltpu.VMEM((16, 2) + slab, BF),
            pltpu.VMEM((NCOL * tile, width), F32),
            pltpu.VMEM((2, 4, 4) + square, BF),
            pltpu.VMEM((2, 4, 4) + square, BF),
            pltpu.VMEM((2, 4) + square, BF),
            pltpu.VMEM((2, 4) + square, BF),
            pltpu.VMEM((2, 4, 4) + square, BF),
            pltpu.VMEM((16,) + slab, F32),
            pltpu.VMEM((16,) + slab, BF),
            pltpu.VMEM((16,) + slab, BF),
            pltpu.VMEM((2, 4) + slab, BF),
            pltpu.VMEM((2, 4) + slab, BF),
            pltpu.VMEM((2, 4) + slab, BF),
            pltpu.VMEM((2, 4) + slab, BF),
            pltpu.VMEM((4, 4) + w_piece, BF),
            pltpu.VMEM((NCOL - 1,) + w_piece, BF),
            pltpu.VMEM((4,) + w_piece, BF),
            pltpu.VMEM((8,) + w_piece, BF),
            pltpu.VMEM((4, 4) + w_piece, BF),
            DMA((7,)),
            DMA((COPIES,)),
            DMA((COPIES,)),
        ],
        compiler_params=pltpu.CompilerParams(
            collective_id=0, has_side_effects=True, vmem_limit_bytes=56 << 20
        ),
        name="layer_backward",
    )(
        tile_coords[0, 0],
        tile_count,
        features,
        weight,
        grad_out,
        tile_values[0, 0],
    )


def solution(mesh):
    return jax.shard_map(
        body,
        mesh=mesh,
        in_specs=(
            P(("col", "row"), None),
            P(),
            P(("col", "row"), None),
            P("col", "row", None, None, None),
            P("col", "row", None, None),
            P("col", "row"),
        ),
        out_specs=(P(("col", "row"), None), P()),
        check_vma=False,
    )
```

```python
import functools
import math

import jax
import jax.numpy as jnp
from jax import lax
from jax.experimental import pallas as pl
from jax.experimental.pallas import tpu as pltpu
from jax.sharding import PartitionSpec as P

MESH = pl.DeviceIdType.MESH
DMA = pltpu.SemaphoreType.DMA
BF = jnp.bfloat16
F32 = jnp.float32

SX, SY, SZ = 4, 4, 16
OFFS = (0, 1, -1, 2, -2, 3, -3, 4, -4, 5, -5, 6, -6, 7, -7, 8)
GROUPS = ((0, 1), (1, 5), (5, 9), (9, 13), (13, 16))
SLOT = {o: t for t, o in enumerate(OFFS)}
SLOT[-8] = SLOT[8]
NCOL = SX * SY


class Links:
    def __init__(self, send_sems, recv_sems):
        self.send_sems, self.recv_sems = send_sems, recv_sems
        self.used = 0
        self.sent = []

    def copy(self, src, dst, device):
        at = self.used
        self.used += 1
        return pltpu.make_async_remote_copy(
            src_ref=src,
            dst_ref=dst,
            send_sem=self.send_sems.at[at],
            recv_sem=self.recv_sems.at[at],
            device_id=device,
            device_id_type=MESH,
        )

    def start(self, src, dst, device):
        copy = self.copy(src, dst, device)
        copy.start()
        self.sent.append(copy)
        return copy

    def drain(self, keep=0):
        cut = len(self.sent) - keep
        for copy in self.sent[:cut]:
            copy.wait_send()
        self.sent = self.sent[cut:]


def kernel(
    pieces,
    chain_pieces,
    scaling,
    coords_ref,
    count_ref,
    feat_ref,
    weight_ref,
    grad_ref,
    tiles_ref,
    out_ref,
    wout_ref,
    coords_s,
    count_s,
    weight_v,
    grad_v,
    inv_v,
    inv_s,
    tiles,
    tiles_t,
    feats,
    acc,
    part,
    part_rx,
    sums,
    sums_rx,
    backs,
    own_t,
    pair_tx,
    pair_rx,
    leaf_tx,
    leaf_rx,
    chain_tx,
    chain_rx,
    w_loc,
    w_rx,
    w_far,
    w_near,
    w_fin,
    local_sems,
    send_sems,
    recv_sems,
):
    col, row = lax.axis_index("col"), lax.axis_index("row")
    x, y = col // SY, col % SY
    z, core = row // 2, row % 2
    links = Links(send_sems, recv_sems)
    slots = tiles_ref.shape[0]
    tile = tiles_ref.shape[1]
    chain_rows = tile // chain_pieces

    def at_z(offset):
        return (col, lax.rem(z + offset + SZ, SZ) * 2 + core)

    def across_z(offset):
        return (col, lax.rem(z + offset + SZ, SZ) * 2 + 1 - core)

    def col_at(dx, dy):
        return lax.rem(x + dx + SX, SX) * SY + lax.rem(y + dy + SY, SY)

    partner = (col, z * 2 + 1 - core)

    def beside(axis, offset):
        return (col_at(offset, 0) if axis == 0 else col_at(0, offset), row)

    barrier = pltpu.get_barrier_semaphore()
    greeted = [at_z(o) for o in (1, -1, 2, -2, 4, -4, 8)] + [partner]
    others = [(d // SY, d % SY) for d in range(NCOL - 1, 0, -1)]
    greeted += [(col_at(dx, dy), row) for dx, dy in others]
    greeted += [across_z(o) for o in (1, -1, 2, -2)]
    for device in greeted:
        pl.semaphore_signal(barrier, inc=1, device_id=device, device_id_type=MESH)

    def load(n, src, dst):
        copy = pltpu.make_async_copy(src, dst, local_sems.at[n])
        copy.start()
        return copy

    load_coords = load(0, coords_ref, coords_s)
    load_count = load(1, count_ref, count_s)
    load_feats = load(2, feat_ref, feats.at[0, 0])
    load_tiles = load(3, tiles_ref, tiles.at[pl.ds(1, slots)])
    load_weight = load(4, weight_ref, weight_v)
    load_grad = load(5, grad_ref, grad_v)

    tile_row = lax.broadcasted_iota(jnp.int32, inv_v.shape, 0)
    tile_col = lax.broadcasted_iota(jnp.int32, inv_v.shape, 1)
    load_coords.wait()
    load_count.wait()
    live = count_s[0, 0]

    def enter(k, table):
        hit = (tile_row == coords_s[0, k]) & (tile_col == coords_s[1, k])
        hit = hit & (jnp.full(inv_v.shape, k, jnp.int32) < live)
        return jnp.where(hit, k + 1, table)

    inv_v[...] = lax.fori_loop(
        0, slots, enter, jnp.zeros(inv_v.shape, jnp.int32), unroll=8
    )
    table_copy = pltpu.make_async_copy(inv_v, inv_s, local_sems.at[6])
    table_copy.start()
    load_feats.wait()
    pl.semaphore_wait(barrier, len(greeted))

    ahead = {}
    rows_of = tile // pieces

    def rows(p):
        return pl.ds(p * rows_of, rows_of)

    def feat_at(t, p):
        return feats.at[t, 0, rows(p)]

    def stride(dist):
        for p in range(pieces):
            for side in (1, -1):
                far = dist + 2
                if dist:
                    ahead[side * dist, p].wait_recv()
                if far == 8 and (p < pieces // 2) != (side == 1):
                    continue
                ahead[side * far, p] = links.start(
                    feat_at(SLOT[side * dist], p),
                    feat_at(SLOT[side * far], p),
                    at_z(side * 2),
                )

    def hand_over(dist):
        for side in (1, -1):
            ahead[side * (dist + 1)] = links.start(
                feats.at[SLOT[side * dist], 0],
                feats.at[SLOT[side * (dist + 1)], 0],
                at_z(side),
            )

    crossed = {}

    def cross(t):
        crossed[t] = links.start(feats.at[t, 0], feats.at[t, 1], partner)

    stride(0)
    hand_over(0)
    cross(0)

    tiles[0] = jnp.zeros(tiles.shape[1:], BF)
    tiles_t[0] = jnp.zeros(tiles.shape[1:], BF)
    table_copy.wait()
    load_tiles.wait()

    def column_tile(t, other):
        source = lax.rem(z - OFFS[t] + SZ, SZ)
        return source * 2 + (1 - core if other else core)

    block = 4

    order = [
        (a + i, b + j) for a, b in ((2, 2), (2, 0), (0, 2), (0, 0)) for i in (0, 1) for j in (0, 1)
    ]

    def row_tile_of(q):
        a = 2 - 2 * (q // 8) + q % 4 // 2
        b = 2 - 2 * (q // 4 % 2) + q % 2
        return lax.rem(x + a, SX) * SY + lax.rem(y + b, SY)

    def product(lo, hi, q0):
        columns = [column_tile(t, o) for t in range(lo, hi) for o in (0, 1)]
        lhs = []
        for a in range(block):
            i = row_tile_of(q0 + a)
            lhs.append(jnp.concatenate([tiles[inv_s[i, j]] for j in columns], axis=1))
        rhs = feats[lo:hi].reshape((hi - lo) * 2 * tile, -1)
        return jnp.dot(
            jnp.concatenate(lhs, axis=0), rhs, preferred_element_type=F32
        )

    def accumulate(lo, hi):
        def one(b, carry):
            at = pl.ds(pl.multiple_of(b * block * tile, block * tile), block * tile)
            if lo == 0:
                acc[at] = product(lo, hi, b * block)
            else:
                acc[at] += product(lo, hi, b * block)
            return carry

        lax.fori_loop(0, NCOL // block, one, 0)

    def flip(k, carry):
        tiles_t[k + 1] = tiles[k + 1].T
        return carry

    lax.fori_loop(0, slots, flip, 0, unroll=4)
    for s in range(1, 5):
        if s < 4:
            stride(2 * s)
            hand_over(2 * s)
        else:
            for p in range(pieces):
                ahead[8 if p < pieces // 2 else -8, p].wait_recv()
        for side in (1, -1):
            if s < 4:
                cross(SLOT[side * 2 * s])
            ahead[side * (2 * s - 1)].wait_recv()
            cross(SLOT[side * (2 * s - 1)])
        if s == 4:
            cross(SLOT[8])
        lo, hi = GROUPS[s - 1]
        for t in range(lo, hi):
            crossed[t].wait_recv()
        accumulate(lo, hi)

    lo, hi = GROUPS[-1]
    for t in range(lo, hi):
        crossed[t].wait_recv()

    lanes = [slice(0, 128), slice(128, 256)]
    first = {}
    for b in range(NCOL // block):
        at = pl.ds(b * block * tile, block * tile)
        total = (acc[at] + product(lo, hi, b * block)).astype(BF)
        some = order[b * block : (b + 1) * block]
        for n, (dx, dy) in enumerate(some):
            for axis, (i, w) in enumerate(((dx, dy), (dy, dx))):
                part[axis, i, w] = total[n * tile : (n + 1) * tile, lanes[axis]]
        for axis in (0, 1):
            for i in sorted({d[axis] for d in some}):
                w = min(d[1 - axis] for d in some)
                if i:
                    first[axis, i, w] = links.start(
                        part.at[axis, i, pl.ds(w, 2)],
                        part_rx.at[axis, i, pl.ds(w, 2)],
                        beside(axis, i),
                    )
    links.drain(12)
    second = {}
    own_sum = {}
    for w0 in (2, 0):
        for axis in (0, 1):
            for i in (1, 2, 3):
                first[axis, i, w0].wait_recv()
            for w in (w0 + 1, w0) if w0 == 0 else (w0, w0 + 1):
                mine = part[axis, 0, w].astype(F32)
                for i in (1, 2, 3):
                    mine = mine + part_rx[axis, i, w].astype(F32)
                if w:
                    sums[axis, w] = mine.astype(BF)
                    second[axis, w] = links.start(
                        sums.at[axis, w], sums_rx.at[axis, w], beside(1 - axis, w)
                    )
                else:
                    own_sum[axis] = mine
    halves = []
    for axis in (0, 1):
        mine = own_sum[axis]
        for w in (2, 3, 1):
            second[axis, w].wait_recv()
            mine = mine + sums_rx[axis, w].astype(F32)
        halves.append(mine)
    agg = jnp.concatenate(halves, axis=1)
    agg = agg.astype(BF)

    load_weight.wait()
    load_grad.wait()
    weight = weight_v[...]
    pre_act = jnp.dot(agg, weight, preferred_element_type=F32)
    sigmoid_z = jax.nn.sigmoid(pre_act)
    factor = sigmoid_z * (1.0 + pre_act * (1.0 - sigmoid_z))
    dz = (grad_v[...].astype(F32) * factor).astype(BF)
    back = lax.dot_general(
        dz, weight, (((1,), (1,)), ((), ())), preferred_element_type=F32
    ).astype(BF)
    for axis in (0, 1):
        backs[axis, 0, 0] = back[:, lanes[axis]]

    for i in (2, 1, 3):
        for axis in (0, 1):
            first[axis, i] = links.start(
                backs.at[axis, 0, 0], backs.at[axis, 0, i], beside(axis, i)
            )
    for w in (2, 1, 3):
        for axis in (0, 1):
            second[axis, w, 0] = links.start(
                backs.at[axis, 0, 0], backs.at[axis, w, 0], beside(1 - axis, w)
            )
    local_weight = lax.dot_general(
        agg, dz, (((0,), (0,)), ((), ())), preferred_element_type=F32
    )
    w_loc[...] = local_weight.astype(BF).reshape(w_loc.shape)
    w_copies = {}
    for n, (dx, dy) in enumerate(others):
        to = (lax.rem(x + dx, SX), lax.rem(y + dy, SY))
        w_copies[n] = links.start(
            w_loc.at[to[0], to[1]], w_rx.at[n], (col_at(dx, dy), row)
        )
    links.drain(27)
    for axis in (0, 1):
        for i in (1, 3, 2):
            first[axis, i].wait_recv()
        for w in (2, 1, 3):
            second[axis, w, 1] = links.start(
                backs.at[axis, 0, pl.ds(1, 3)],
                backs.at[axis, w, pl.ds(1, 3)],
                beside(1 - axis, w),
            )

    w_own = w_loc[x, y].astype(F32)
    for n in range(len(others)):
        w_copies[n].wait_recv()
        w_own = w_own + w_rx[n].astype(F32)
    group, place = z // 4, z % 4
    w_far[group] = w_own.astype(BF)
    for i in (8, 4, -4):
        w_copies[i] = links.start(w_far.at[group], w_far.at[group], at_z(i))

    links.drain(9)
    for axis in (0, 1):
        for w in (1, 3, 2):
            second[axis, w, 0].wait_recv()
            second[axis, w, 1].wait_recv()

    def back_tile_of(d):
        return lax.rem(x - d // SY + SX, SX) * SY + lax.rem(y - d % SY + SY, SY)

    def whole_back():
        left = [backs[0, d % SY, d // SY] for d in range(NCOL)]
        right = [backs[1, d // SY, d % SY] for d in range(NCOL)]
        return jnp.concatenate(
            [jnp.concatenate(left, axis=0), jnp.concatenate(right, axis=0)], axis=1
        )

    def transposed(columns):
        lhs = []
        for j in columns:
            lhs.append(
                jnp.concatenate(
                    [tiles_t[inv_s[back_tile_of(d), j]] for d in range(NCOL)], axis=1
                )
            )
        return jnp.dot(
            jnp.concatenate(lhs, axis=0),
            whole_back(),
            preferred_element_type=F32,
        )

    pair = {}

    def compute(offsets):
        for t0 in range(0, len(offsets), 2):
            some = offsets[t0 : t0 + 2]
            targets = [lax.rem(z + o + SZ, SZ) * 2 for o in some]
            terms = transposed(
                [t + 1 - core for t in targets] + [t + core for t in targets]
            )
            for n, o in enumerate(some):
                t = SLOT[o]
                pair_tx[t] = terms[n * tile : (n + 1) * tile].astype(BF)
                pair[t] = links.start(pair_tx.at[t], pair_rx.at[t], partner)
                m = n + len(some)
                own_t[t] = terms[m * tile : (m + 1) * tile]

    def pair_sum(o):
        t = SLOT[o]
        pair[t].wait_recv()
        return own_t[t] + pair_rx[t].astype(F32)

    leaf, chain = {}, {}

    def send_leaves(dist):
        for n, side in enumerate((1, -1)):
            m = dist // 2
            leaf_tx[n, m] = pair_sum(side * dist).astype(BF)
            leaf[side, dist] = links.start(
                leaf_tx.at[n, m], leaf_rx.at[n, m], at_z(side)
            )

    def send_chain(dist):
        m = dist // 2 - 1
        totals = []
        for n, side in enumerate((1, -1)):
            if dist == 8:
                totals.append(totals[0] if n else pair_sum(8))
            else:
                total = pair_sum(side * dist)
                leaf[side, dist + 1].wait_recv()
                totals.append(total + leaf_rx[n, m + 1].astype(F32))
        apart = chain_pieces // 2
        for turn in range(apart if dist == 8 else chain_pieces):
            for n, side in enumerate((1, -1)):
                h = (n * apart + turn) % chain_pieces
                at = pl.ds(h * chain_rows, chain_rows)
                mine = totals[n][h * chain_rows : (h + 1) * chain_rows]
                if dist < 6 or dist == 6 and turn < apart:
                    chain[side, dist + 2, h].wait_recv()
                    mine = mine + chain_rx[n, m + 1, at].astype(F32)
                chain_tx[n, m, at] = mine.astype(BF)
                chain[side, dist, h] = links.start(
                    chain_tx.at[n, m, at], chain_rx.at[n, m, at], at_z(2 * side)
                )

    compute([8])
    compute([7, -7])
    send_chain(8)
    compute([6, -6])
    send_leaves(7)
    compute([5, -5])
    compute([4, -4])
    send_leaves(5)
    compute([3, -3])
    send_chain(6)
    send_leaves(3)
    for i in (8, 4, -4):
        w_copies[i].wait_recv()
    mine = place * 2 + core
    w_near[mine] = jnp.sum(w_far[...].astype(F32), axis=0).astype(BF)
    for n, device in enumerate(
        [f(o) for o in (2, 1, -1) for f in (at_z, across_z)] + [partner]
    ):
        w_copies[n] = links.start(w_near.at[mine], w_near.at[mine], device)
    compute([2, -2])
    compute([1, -1])
    compute([0])
    send_leaves(1)
    links.drain(20)
    send_chain(4)
    for n in range(7):
        w_copies[n].wait_recv()
    w_fin[x, y] = (jnp.sum(w_near[...].astype(F32), axis=0) * scaling).astype(BF)
    for n, (dx, dy) in enumerate(others):
        w_copies[n] = links.start(
            w_fin.at[x, y], w_fin.at[x, y], (col_at(dx, dy), row)
        )
    links.drain(15 + 2 * chain_pieces)
    send_chain(2)
    links.drain(2 * chain_pieces)
    total = pair_sum(0)
    for n, side in enumerate((1, -1)):
        leaf[side, 1].wait_recv()
        total = total + leaf_rx[n, 0].astype(F32)
    for n, side in enumerate((1, -1)):
        for h in range(chain_pieces):
            chain[side, 2, h].wait_recv()
        total = total + chain_rx[n, 0].astype(F32)
    out_ref[...] = total.astype(BF)
    for n in range(len(others)):
        w_copies[n].wait_recv()
    wout_ref[...] = w_fin[...].astype(F32).reshape(wout_ref.shape)
    links.drain()


PIECES = 4
CHAIN_PIECES = 2
COPIES = 192


def body(features, weight, grad_out, tile_values, tile_coords, tile_count):
    tile, width = features.shape
    slots = tile_values.shape[2]
    nodes = tile * lax.axis_size("col") * lax.axis_size("row")
    vmem = pl.BlockSpec(memory_space=pltpu.VMEM)
    square = (tile, tile)
    slab = (tile, width)
    w_piece = (width // NCOL, width)
    return pl.pallas_call(
        functools.partial(kernel, PIECES, CHAIN_PIECES, 1.0 / math.sqrt(nodes)),
        out_shape=(pltpu.VMEM(slab, BF), pltpu.VMEM((width, width), F32)),
        in_specs=[pl.BlockSpec(memory_space=pltpu.HBM)] * 6,
        out_specs=(vmem, vmem),
        scratch_shapes=[
            pltpu.SMEM((2, slots), jnp.int32),
            pltpu.SMEM((1, 1), jnp.int32),
            pltpu.VMEM((width, width), BF),
            pltpu.VMEM(slab, BF),
            pltpu.VMEM((16, 128), jnp.int32),
            pltpu.SMEM((16, 128), jnp.int32),
            pltpu.VMEM((slots + 1,) + square, BF),
            pltpu.VMEM((slots + 1,) + square, BF),
            pltpu.VMEM((16, 2) + slab, BF),
            pltpu.VMEM((NCOL * tile, width), F32),
            pltpu.VMEM((2, 4, 4) + square, BF),
            pltpu.VMEM((2, 4, 4) + square, BF),
            pltpu.VMEM((2, 4) + square, BF),
            pltpu.VMEM((2, 4) + square, BF),
            pltpu.VMEM((2, 4, 4) + square, BF),
            pltpu.VMEM((16,) + slab, F32),
            pltpu.VMEM((16,) + slab, BF),
            pltpu.VMEM((16,) + slab, BF),
            pltpu.VMEM((2, 4) + slab, BF),
            pltpu.VMEM((2, 4) + slab, BF),
            pltpu.VMEM((2, 4) + slab, BF),
            pltpu.VMEM((2, 4) + slab, BF),
            pltpu.VMEM((4, 4) + w_piece, BF),
            pltpu.VMEM((NCOL - 1,) + w_piece, BF),
            pltpu.VMEM((4,) + w_piece, BF),
            pltpu.VMEM((8,) + w_piece, BF),
            pltpu.VMEM((4, 4) + w_piece, BF),
            DMA((7,)),
            DMA((COPIES,)),
            DMA((COPIES,)),
        ],
        compiler_params=pltpu.CompilerParams(
            collective_id=0, has_side_effects=True, vmem_limit_bytes=56 << 20
        ),
        name="layer_backward",
    )(
        tile_coords[0, 0],
        tile_count,
        features,
        weight,
        grad_out,
        tile_values[0, 0],
    )


def solution(mesh):
    return jax.shard_map(
        body,
        mesh=mesh,
        in_specs=(
            P(("col", "row"), None),
            P(),
            P(("col", "row"), None),
            P("col", "row", None, None, None),
            P("col", "row", None, None),
            P("col", "row"),
        ),
        out_specs=(P(("col", "row"), None), P()),
        check_vma=False,
    )
```
